256 devices in a mesh: seg: 32 (over x, z), head: 8 (over y, core).
Axes of the slice: x: 4, y: 4, z: 8, core: 2. Of those that a mesh axis runs over, the one named last changes fastest.
Arguments:
- q_heads: bfloat16 [24576, 4096], P('seg', 'head'), may hold values from -6 to 6
- k_heads: bfloat16 [24576, 4096], P('seg', 'head'), may hold values from -6 to 6
- v_heads: bfloat16 [24576, 4096], P('seg', 'head'), may hold values from -600 to 600
- log_decay: float32 [32, 24576], P('head', 'seg'), may hold values from -1 to 0
- parent: int32 [32], replicated, may hold values from -1 to 31, as said below
- norm_gain: float32 [4096], P('head'), may hold values from 0.1 to 1.9
- w_out: bfloat16 [4096, 6144], P('head'), may hold values from -0.09375 to 0.09375
Outputs:
- mixed: bfloat16 [24576, 6144], P(('seg', 'head'))
The draws below stay inside these ranges and needn't reach their ends.
Inputs may be any that keep to these rules, and one draw needn't show every extreme that they name: A segment's parent is a root or a segment whose parent is a root; the tree has three levels, and the third is never empty.
All inputs are finite; a program needn't handle non-finite values.
Results may differ from the reference program's by a relative error of at most 0.0051.
Values sent between devices are 32-bit elements; how exact they have to be, the bound alone decides.
No kernel may reach another device: no remote copies, remote signals or barrier semaphores. Data moves between devices by JAX's collectives and lax.ppermute only.
A program may use at most 128 MiB of HBM per device.

```python
import math
import jax
import jax.numpy as jnp
from jax import lax

HID = 6144
DH = 128
SEGMENT_LENGTH = 768
HEAD_TOTAL = 32
FEAT = 4096
NSEG = 32
TOKEN_TOTAL = 24576


def draw_parent(key, part):
    key_order = jax.random.fold_in(key, 101)
    key_root = jax.random.fold_in(key, 102)
    key_middle = jax.random.fold_in(key, 103)
    rest = jax.random.permutation(key_order, NSEG - 1).astype(jnp.int32)
    order = jnp.concatenate([jnp.full((1,), NSEG - 1, jnp.int32), rest]).astype(jnp.int32)
    first = max(NSEG // 8, 1)
    second = first + max(NSEG * 3 // 8, 1)
    rank = jnp.arange(NSEG, dtype=jnp.int32)
    pick_root = jax.random.randint(key_root, (NSEG,), 0, first)
    pick_root = jnp.where(rank == first, 0, pick_root)
    pick_middle = jax.random.randint(key_middle, (NSEG,), first, second)
    pick_middle = jnp.where(rank == second, first, pick_middle)
    by_rank = jnp.where(rank < first, -1, jnp.where(rank < second, order[pick_root], order[pick_middle]))
    return jnp.zeros((NSEG,), jnp.int32).at[order].set(by_rank.astype(jnp.int32))


def draw_log_decay(key, part):
    key_fast = jax.random.fold_in(key, 201)
    key_slow = jax.random.fold_in(key, 202)
    key_quick = jax.random.fold_in(key, 203)
    key_segment = jax.random.fold_in(key, 204)
    key_rough = jax.random.fold_in(key, 205)
    key_spike_seed = jax.random.fold_in(key, 206)
    key_loss = jax.random.fold_in(key, 207)
    chain = 3.0 * SEGMENT_LENGTH
    share = 0.5
    fast = (jax.random.uniform(key_fast, (HEAD_TOTAL, 1, 1)) < share).astype(jnp.float32)
    slow_rate = jnp.exp(jax.random.uniform(key_slow, (HEAD_TOTAL, 1, 1), minval=math.log(0.05), maxval=math.log(0.5))) / chain
    quick_rate = jnp.exp(jax.random.uniform(key_quick, (HEAD_TOTAL, 1, 1), minval=math.log(1.0 / 50.0), maxval=math.log(1.0 / 30.0)))
    rate = fast * quick_rate + (1.0 - fast) * slow_rate
    segment_factor = jnp.exp(jax.random.uniform(key_segment, (HEAD_TOTAL, NSEG, 1), minval=math.log(0.5), maxval=0.0))
    rough = jax.random.uniform(key_rough, (HEAD_TOTAL, NSEG, SEGMENT_LENGTH), minval=0.5, maxval=1.5)
    stable_level = (rate * segment_factor * rough).reshape(HEAD_TOTAL, TOKEN_TOTAL)
    sudden_spike = jax.random.uniform(key_spike_seed, (HEAD_TOTAL, TOKEN_TOTAL)) < 1.0 / SEGMENT_LENGTH
    training_loss = jnp.log(jax.random.uniform(key_loss, (HEAD_TOTAL, TOKEN_TOTAL), minval=0.5, maxval=0.8))
    return (-stable_level + jnp.where(sudden_spike, training_loss, 0.0)).astype(jnp.float32)


def draw_v_heads(key, part):
    key_base = jax.random.fold_in(key, 301)
    key_row = jax.random.fold_in(key, 302)
    key_head = jax.random.fold_in(key, 303)
    base = jnp.clip(jax.random.normal(key_base, (TOKEN_TOTAL, FEAT)), -6.0, 6.0)
    row_scale = jnp.exp(jax.random.uniform(key_row, (TOKEN_TOTAL, 1), minval=0.0, maxval=math.log(10.0)))
    head_index = jnp.arange(FEAT) // DH
    rising = 3.0 ** (head_index.astype(jnp.float32) / max(HEAD_TOTAL - 1, 1))
    spread = jnp.exp(jax.random.uniform(key_head, (HEAD_TOTAL,), minval=0.0, maxval=math.log(3.3)))[head_index]
    return jnp.clip(base * row_scale * rising * spread, -600.0, 600.0).astype(jnp.bfloat16)


def level_of(key, dims, shards, least, top_value):
    def one(dim, parts):
        steps = jax.random.uniform(jax.random.fold_in(jax.random.fold_in(key, 6), dim), (parts,), jnp.float32, least / len(shards), top_value / len(shards))
        return jnp.repeat(jnp.exp(steps), dims[dim] // parts).reshape((-1,) + (1,) * (len(dims) - dim - 1))

    level = one(*shards[0])
    for cut in shards[1:]:
        level = level * one(*cut)
    return level


def noise(own_key, extent, scale, limit, pieces=(), held_as=jnp.bfloat16):
    loudness = level_of(own_key, extent, pieces, -0.22, 0.18) if pieces else 1.0
    values = jax.random.normal(own_key, extent, jnp.float32) * scale * loudness
    return jnp.minimum(jnp.maximum(values, -limit), limit).astype(held_as)


def setup_inputs(seed: int = 0) -> dict:
    keys = jax.random.split(jax.random.key(seed), 8)
    return {
        "q_heads": noise(keys[0], (TOKEN_TOTAL, FEAT), 1.0, 6.0, ((0, 32), (1, 8))),
        "k_heads": noise(keys[1], (TOKEN_TOTAL, FEAT), 1.0, 6.0, ((0, 32), (1, 8))),
        "v_heads": draw_v_heads(jax.random.fold_in(keys[7], 71), 0),
        "log_decay": draw_log_decay(jax.random.fold_in(keys[7], 71), 0),
        "parent": draw_parent(jax.random.fold_in(keys[7], 71), 0),
        "norm_gain": jnp.clip(1.0 + 0.18 * jax.random.normal(keys[5], (FEAT,), jnp.float32), 0.1, 1.9),
        "w_out": noise(keys[6], (FEAT, HID), FEAT ** -0.5, 0.09375, ((0, 8),)),
    }


def segment_state(key_rows, values, decay_logs):
    running = jnp.cumsum(decay_logs, axis=1)
    segment_total = running[:, -1]
    key_weight = jnp.exp(segment_total[:, None] - running)
    weighted = key_rows.astype(jnp.float32) * key_weight.T[:, :, None]
    local_state = jnp.einsum('shd,she->hde', weighted, values.astype(jnp.float32), precision=lax.Precision.HIGHEST)
    return (running, local_state, segment_total)

def segment_output(queries, key_rows, values, running, prefix):
    length = queries.shape[0]
    scale = DH ** (-0.5)
    scores = jnp.einsum('thd,shd->hts', queries.astype(jnp.float32), key_rows.astype(jnp.float32), precision=lax.Precision.HIGHEST)
    row_index = lax.broadcasted_iota(jnp.int32, (length, length), 0)
    col_index = lax.broadcasted_iota(jnp.int32, (length, length), 1)
    causal = row_index >= col_index
    log_gap = running[:, :, None] - running[:, None, :]
    decay_factor = jnp.where(causal[None], jnp.exp(jnp.minimum(log_gap, 0.0)), 0.0)
    weights = (scores * scale * decay_factor).astype(jnp.bfloat16)
    within = jnp.einsum('hts,she->the', weights.astype(jnp.float32), values.astype(jnp.float32), precision=lax.Precision.HIGHEST)
    prefix_term = jnp.einsum('thd,hde->the', queries.astype(jnp.float32), prefix, precision=lax.Precision.HIGHEST) * jnp.exp(running).T[:, :, None]
    return prefix_term + within

def reference(q_heads, k_heads, v_heads, log_decay, parent, norm_gain, w_out):
    queries = q_heads.reshape(NSEG, SEGMENT_LENGTH, HEAD_TOTAL, DH)
    key_rows = k_heads.reshape(NSEG, SEGMENT_LENGTH, HEAD_TOTAL, DH)
    values = v_heads.reshape(NSEG, SEGMENT_LENGTH, HEAD_TOTAL, DH)
    decays = log_decay.reshape(HEAD_TOTAL, NSEG, SEGMENT_LENGTH).transpose(1, 0, 2)
    running, local_state, segment_total = lax.map(lambda items: segment_state(*items), (key_rows, values, decays))
    has_parent = parent >= 0
    parent_index = jnp.maximum(parent, 0).astype(jnp.int32)
    end_state = local_state
    prefix = jnp.zeros_like(local_state)
    for step_index in range(2):
        prefix = jnp.where(has_parent[:, None, None, None], end_state[parent_index], jnp.float32(0.0))
        end_state = jnp.exp(segment_total)[:, :, None, None] * prefix + local_state
    attention = lax.map(lambda items: segment_output(*items), (queries, key_rows, values, running, prefix))
    attention = attention.reshape(TOKEN_TOTAL, FEAT)
    squares = lax.optimization_barrier(jnp.sum(attention * attention, axis=1))
    inverse = 1.0 / jnp.sqrt(squares / FEAT + 1e-06)
    normed = (attention * inverse[:, None] * norm_gain[None, :]).astype(jnp.bfloat16)
    return jnp.dot(normed, w_out, preferred_element_type=jnp.float32).astype(jnp.bfloat16)
```

```python
import functools
import jax
import jax.numpy as jnp
from jax import lax
from jax.experimental import pallas as pl
from jax.experimental.pallas import tpu as pltpu
from jax.sharding import PartitionSpec as P

F32, BF16 = jnp.float32, jnp.bfloat16
NT = (((1,), (1,)), ((), ()))
TN = (((0,), (0,)), ((), ()))
NN = (((1,), (0,)), ((), ()))


def dot(a, b, dims=NN):
    return lax.dot_general(a, b, dims, preferred_element_type=F32)


def split(x):
    high = x.astype(BF16)
    return high, (x - high.astype(F32)).astype(BF16)


def state_kernel(decay_ref, k_ref, v_ref, chunks_ref, running_ref, column_ref):
    heads, length = decay_ref.shape
    running = jnp.concatenate([decay_ref[...]] * (8 // heads), axis=0)
    lane = lax.broadcasted_iota(jnp.int32, running.shape, 1)
    shift = 1
    while shift < length:
        running += jnp.where(lane >= shift, pltpu.roll(running, shift, 1), 0.0)
        shift *= 2
    running_ref[...] = running
    column = running.T
    column_ref[...] = column
    for h in range(heads):
        cols = slice(128 * h, 128 * h + 128)
        total = column[length - 1 : length, h : h + 1]
        weight = jnp.exp(total - column[:, h : h + 1])
        high, low = split(k_ref[:, cols].astype(F32) * weight)
        values = v_ref[:, cols]
        state = dot(high, values, TN) + dot(low, values, TN)
        chunks_ref[8 * h : 8 * h + 8, 0:16, :] = state.reshape(8, 16, 128)
        chunks_ref[8 * h : 8 * h + 8, 16:24, :] = jnp.broadcast_to(total.reshape(1, 1, 1), (8, 8, 128))


def prefix_kernel(parent_ref, all_ref, out_ref):
    segments = all_ref.shape[0]

    def body(s, carry):
        first = parent_ref[s]
        p = jnp.clip(first, 0, segments - 1)
        second = parent_ref[p]
        g = jnp.clip(second, 0, segments - 1)
        own = all_ref[p, 0:16, :]
        factor = jnp.exp(all_ref[p, 16:24, :])
        factor = jnp.concatenate([factor, factor], axis=0)
        older = jnp.where(second >= 0, factor * all_ref[g, 0:16, :], 0.0)
        out_ref[s] = jnp.where(first >= 0, own + older, 0.0)
        return carry

    lax.fori_loop(0, segments, body, 0)


def within_kernel(q_ref, k_ref, v_ref, running_ref, column_ref, out_ref):
    length = q_ref.shape[0]
    size = 256
    scale = 128 ** (-0.5)
    causal = lax.broadcasted_iota(jnp.int32, (size, size), 0) >= lax.broadcasted_iota(jnp.int32, (size, size), 1)
    for h in range(4):
        cols = slice(128 * h, 128 * h + 128)
        for i in range(length // size):
            rows = slice(size * i, size * i + size)
            q = q_ref[rows, cols]
            total = None
            for j in range(i + 1):
                inner = slice(size * j, size * j + size)
                scores = dot(q, k_ref[inner, cols], NT)
                gap = column_ref[rows, h : h + 1] - running_ref[h : h + 1, inner]
                factor = jnp.exp(jnp.minimum(gap, 0.0))
                if i == j:
                    factor = jnp.where(causal, factor, 0.0)
                weights = (scores * scale * factor).astype(BF16)
                term = dot(weights, v_ref[inner, cols])
                total = term if total is None else total + term
            out_ref[rows, cols] = total


def mix_kernel(q_ref, prefix_ref, within_ref, column_ref, gain_ref, out_ref, squares_ref):
    squares = None
    for h in range(4):
        cols = slice(128 * h, 128 * h + 128)
        high, low = split(prefix_ref[h])
        q = q_ref[:, cols]
        grown = (dot(q, high) + dot(q, low)) * jnp.exp(column_ref[:, h : h + 1])
        attention = grown + within_ref[:, cols]
        term = jnp.sum(attention * attention, axis=1, keepdims=True)
        squares = term if squares is None else squares + term
        out_ref[:, cols] = (attention * gain_ref[:, cols]).astype(BF16)
    squares_ref[...] = jnp.broadcast_to(squares, squares_ref.shape)


VMEM = pl.BlockSpec(memory_space=pltpu.VMEM)
SMEM = pl.BlockSpec(memory_space=pltpu.SMEM)


def call(kernel, shapes, count, scalars=0, flops=0):
    return pl.pallas_call(
        kernel,
        out_shape=[jax.ShapeDtypeStruct(s, d) for s, d in shapes],
        in_specs=[SMEM] * scalars + [VMEM] * (count - scalars),
        out_specs=[VMEM] * len(shapes),
        compiler_params=pltpu.CompilerParams(vmem_limit_bytes=48 * 2**20),
        cost_estimate=pl.CostEstimate(flops=flops, bytes_accessed=6 * 2**20, transcendentals=0),
    )


def per_device(q, k, v, log_decay, parent, gain, w):
    length, width = q.shape
    chunks, running, column = call(
        state_kernel, [((32, 24, 128), F32), ((8, length), F32), ((length, 8), F32)], 3, flops=2**28
    )(log_decay, k, v)
    everyone = lax.all_to_all(chunks, "seg", 0, 0, tiled=True)
    (within,) = call(within_kernel, [((length, width), F32)], 5, flops=2**31)(q, k, v, running, column)
    (mine,) = call(prefix_kernel, [((32, 16, 128), F32)], 2, scalars=1)(parent, everyone)
    prefix = lax.all_to_all(mine, "seg", 0, 0, tiled=True).reshape(4, 128, 128)
    features, squares = call(mix_kernel, [((length, width), BF16), ((length, 128), F32)], 5, flops=2**28)(
        q, prefix, within, column, gain.reshape(1, width)
    )
    part = jnp.dot(features, w, preferred_element_type=F32)
    mixed = lax.psum_scatter(part, "head", scatter_dimension=0, tiled=True)
    squares = lax.psum_scatter(squares, "head", scatter_dimension=0, tiled=True)
    inverse = 1.0 / jnp.sqrt(squares[:, :1] / (width * lax.axis_size("head")) + 1e-06)
    return (mixed * inverse).astype(BF16)


def solution(mesh):
    return jax.shard_map(
        per_device,
        mesh=mesh,
        in_specs=(P("seg", "head"), P("seg", "head"), P("seg", "head"), P("head", "seg"), P(), P("head"), P("head", None)),
        out_specs=P(("seg", "head"), None),
        check_vma=False,
    )
```

```python
import functools
import jax
import jax.numpy as jnp
from jax import lax
from jax.experimental import pallas as pl
from jax.experimental.pallas import tpu as pltpu
from jax.sharding import PartitionSpec as P

F32, BF16 = jnp.float32, jnp.bfloat16
NT = (((1,), (1,)), ((), ()))
TN = (((0,), (0,)), ((), ()))
NN = (((1,), (0,)), ((), ()))


def dot(a, b, dims=NN):
    return lax.dot_general(a, b, dims, preferred_element_type=F32)


def split(x):
    high = x.astype(BF16)
    return high, (x - high.astype(F32)).astype(BF16)


def state_kernel(decay_ref, k_ref, v_ref, chunks_ref, running_ref, column_ref):
    heads, length = decay_ref.shape
    running = jnp.concatenate([decay_ref[...]] * (8 // heads), axis=0)
    lane = lax.broadcasted_iota(jnp.int32, running.shape, 1)
    shift = 1
    while shift < length:
        running += jnp.where(lane >= shift, pltpu.roll(running, shift, 1), 0.0)
        shift *= 2
    running_ref[...] = running
    column = running.T
    column_ref[...] = column
    for h in range(heads):
        cols = slice(128 * h, 128 * h + 128)
        total = column[length - 1 : length, h : h + 1]
        weight = jnp.exp(total - column[:, h : h + 1])
        high, low = split(k_ref[:, cols].astype(F32) * weight)
        values = v_ref[:, cols]
        state = dot(high, values, TN) + dot(low, values, TN)
        chunks_ref[8 * h : 8 * h + 8, 0:16, :] = state.reshape(8, 16, 128)
        chunks_ref[8 * h : 8 * h + 8, 16:24, :] = jnp.broadcast_to(total.reshape(1, 1, 1), (8, 8, 128))


def prefix_kernel(parent_ref, all_ref, out_ref):
    segments = all_ref.shape[0]

    def body(s, carry):
        first = parent_ref[s]
        p = jnp.clip(first, 0, segments - 1)
        second = parent_ref[p]
        g = jnp.clip(second, 0, segments - 1)
        own = all_ref[p, 0:16, :]
        factor = jnp.exp(all_ref[p, 16:24, :])
        factor = jnp.concatenate([factor, factor], axis=0)
        older = jnp.where(second >= 0, factor * all_ref[g, 0:16, :], 0.0)
        out_ref[s] = jnp.where(first >= 0, own + older, 0.0)
        return carry

    lax.fori_loop(0, segments, body, 0)


def within_kernel(q_ref, k_ref, v_ref, running_ref, column_ref, out_ref):
    length = q_ref.shape[0]
    size = 256
    scale = 128 ** (-0.5)
    causal = lax.broadcasted_iota(jnp.int32, (size, size), 0) >= lax.broadcasted_iota(jnp.int32, (size, size), 1)
    for h in range(4):
        cols = slice(128 * h, 128 * h + 128)
        for i in range(length // size):
            rows = slice(size * i, size * i + size)
            q = q_ref[rows, cols]
            total = None
            for j in range(i + 1):
                inner = slice(size * j, size * j + size)
                scores = dot(q, k_ref[inner, cols], NT)
                gap = column_ref[rows, h : h + 1] - running_ref[h : h + 1, inner]
                factor = jnp.exp(jnp.minimum(gap, 0.0))
                if i == j:
                    factor = jnp.where(causal, factor, 0.0)
                weights = (scores * scale * factor).astype(BF16)
                term = dot(weights, v_ref[inner, cols])
                total = term if total is None else total + term
            out_ref[rows, cols] = total


def mix_kernel(q_ref, prefix_ref, within_ref, column_ref, gain_ref, out_ref, squares_ref):
    squares = None
    for h in range(4):
        cols = slice(128 * h, 128 * h + 128)
        high, low = split(prefix_ref[h])
        q = q_ref[:, cols]
        grown = (dot(q, high) + dot(q, low)) * jnp.exp(column_ref[:, h : h + 1])
        attention = grown + within_ref[:, cols]
        term = jnp.sum(attention * attention, axis=1, keepdims=True)
        squares = term if squares is None else squares + term
        out_ref[:, cols] = (attention * gain_ref[:, cols]).astype(BF16)
    squares_ref[...] = jnp.broadcast_to(squares, (squares.shape[0], 128)).T[0:8, :]


def project_kernel(index_ref, own_ref, other_ref, w_ref, keep_ref, send_ref):
    keep_ref[...] = dot(own_ref[0], w_ref[...])
    send_ref[...] = dot(other_ref[0], w_ref[...])


def project(blocks, step, features, w, start, width):
    rows, depth = features.shape[1:]
    tile = 1024
    out = pl.BlockSpec((rows, tile), lambda n, index: (0, n))
    return pl.pallas_call(
        project_kernel,
        out_shape=[jax.ShapeDtypeStruct((rows, width), F32)] * 2,
        grid_spec=pltpu.PrefetchScalarGridSpec(
            num_scalar_prefetch=1,
            grid=(width // tile,),
            in_specs=[
                pl.BlockSpec((1, rows, depth), lambda n, index: (index[2 * step], 0, 0)),
                pl.BlockSpec((1, rows, depth), lambda n, index: (index[2 * step + 1], 0, 0)),
                pl.BlockSpec((depth, tile), lambda n, index: (0, start // tile + n)),
            ],
            out_specs=[out, out],
        ),
        compiler_params=pltpu.CompilerParams(vmem_limit_bytes=16 * 2**20),
        cost_estimate=pl.CostEstimate(flops=4 * rows * depth * width, bytes_accessed=8 * rows * width, transcendentals=0),
    )(blocks, features, features, w)


def finish_kernel(inverse_ref, *refs):
    terms, out_ref = refs[:3], refs[-1]
    out_ref[...] = ((terms[0][...] + terms[1][...] + terms[2][...]) * inverse_ref[...]).astype(BF16)


def finish(inverse, terms, start, columns, out):
    rows, width = terms[0].shape
    tile = 1024
    block = pl.BlockSpec((rows, tile), lambda n: (0, n))
    args = [inverse, *terms] + ([] if out is None else [out])
    return pl.pallas_call(
        finish_kernel,
        out_shape=jax.ShapeDtypeStruct((rows, columns), BF16),
        grid=(width // tile,),
        in_specs=[pl.BlockSpec((rows, 1), lambda n: (0, 0))] + [block] * 3 + [pl.BlockSpec(memory_space=pl.ANY)] * (out is not None),
        out_specs=pl.BlockSpec((rows, tile), lambda n: (0, start // tile + n)),
        input_output_aliases={} if out is None else {4: 0},
        compiler_params=pltpu.CompilerParams(vmem_limit_bytes=16 * 2**20),
        cost_estimate=pl.CostEstimate(flops=4 * rows * width, bytes_accessed=14 * rows * width, transcendentals=0),
    )(*args)


def head_pairs(target):
    pairs = []
    for y in range(4):
        for core in range(2):
            to, to_core = target(y, core)
            pairs.append((2 * y + core, 2 * (to % 4) + to_core))
    return pairs


SWAP = head_pairs(lambda y, core: (y, 1 - core))
RING = head_pairs(lambda y, core: (y + 1 - 2 * core, core))
NEAR = head_pairs(lambda y, core: (y ^ 1, core))
FAR = head_pairs(lambda y, core: (y ^ 2, core))


VMEM = pl.BlockSpec(memory_space=pltpu.VMEM)
SMEM = pl.BlockSpec(memory_space=pltpu.SMEM)


def call(kernel, shapes, count, scalars=0, flops=0):
    return pl.pallas_call(
        kernel,
        out_shape=[jax.ShapeDtypeStruct(s, d) for s, d in shapes],
        in_specs=[SMEM] * scalars + [VMEM] * (count - scalars),
        out_specs=[VMEM] * len(shapes),
        compiler_params=pltpu.CompilerParams(vmem_limit_bytes=16 * 2**20),
        cost_estimate=pl.CostEstimate(flops=flops, bytes_accessed=6 * 2**20, transcendentals=0),
    )


def per_device(q, k, v, log_decay, parent, gain, w):
    length, width = q.shape
    chunks, running, column = call(
        state_kernel, [((32, 24, 128), F32), ((8, length), F32), ((length, 8), F32)], 3, flops=2**28
    )(log_decay, k, v)
    everyone = lax.all_to_all(chunks, "seg", 0, 0, tiled=True)
    (within,) = call(within_kernel, [((length, width), F32)], 5, flops=2**31)(q, k, v, running, column)
    (mine,) = call(prefix_kernel, [((32, 16, 128), F32)], 2, scalars=1)(parent, everyone)
    prefix = lax.all_to_all(mine, "seg", 0, 0, tiled=True).reshape(4, 128, 128)
    features, squares = call(mix_kernel, [((length, width), BF16), ((8, length), F32)], 5, flops=2**28)(
        q, prefix, within, column, gain.reshape(1, width)
    )
    for pairs in (SWAP, NEAR, FAR):
        squares = squares + lax.ppermute(squares, "head", pairs)
    me = lax.axis_index("head")
    y, core = me >> 1, me & 1
    way = (1 - 2 * core) * jnp.arange(1, 5, dtype=jnp.int32)
    blocks = jnp.stack([((y - way) & 3) * 2 + core, ((y + way) & 3) * 2 + 1 - core], axis=1).reshape(8)
    share = length // 8
    features = features.reshape(8, share, width)
    chunks = 2
    part = w.shape[1] // chunks
    arrived = [None] * chunks
    for step in range(1, 5):
        for chunk in range(chunks):
            keep, send = project(blocks, step - 1, features, w, chunk * part, part)
            terms = [keep, lax.ppermute(send, "head", SWAP)] + ([arrived[chunk]] if step > 1 else [])
            arrived[chunk] = lax.ppermute(sum(terms[1:], terms[0]), "head", RING) if step < 4 else terms
    squares = lax.dynamic_index_in_dim(squares[0].reshape(8, share), me, 0, keepdims=False)
    inverse = 1.0 / jnp.sqrt(squares / (width * lax.axis_size("head")) + 1e-06)
    out = None
    for chunk in range(chunks):
        out = finish(inverse[:, None], arrived[chunk], chunk * part, w.shape[1], out)
    return out


def solution(mesh):
    return jax.shard_map(
        per_device,
        mesh=mesh,
        in_specs=(P("seg", "head"), P("seg", "head"), P("seg", "head"), P("head", "seg"), P(), P("head"), P("head", None)),
        out_specs=P(("seg", "head"), None),
        check_vma=False,
    )
```

```python
import functools
import jax
import jax.numpy as jnp
from jax import lax
from jax.experimental import pallas as pl
from jax.experimental.pallas import tpu as pltpu
from jax.sharding import PartitionSpec as P

F32, BF16 = jnp.float32, jnp.bfloat16
NT = (((1,), (1,)), ((), ()))
TN = (((0,), (0,)), ((), ()))
NN = (((1,), (0,)), ((), ()))


def dot(a, b, dims=NN):
    return lax.dot_general(a, b, dims, preferred_element_type=F32)


def split(x):
    high = x.astype(BF16)
    return high, (x - high.astype(F32)).astype(BF16)


def load(sems, *pairs):
    copies = [pltpu.make_async_copy(source, target, sems.at[i]) for i, (source, target) in enumerate(pairs)]
    for copy in copies:
        copy.start()
    return copies


def state_kernel(decay_hbm, k_hbm, v_hbm, chunks_ref, running_ref, decay_ref, k_ref, v_ref, sems):
    copies = load(sems, (decay_hbm, decay_ref), (k_hbm, k_ref), (v_hbm, v_ref))
    copies[0].wait()
    heads, length = decay_ref.shape
    running = jnp.concatenate([decay_ref[...]] * (8 // heads), axis=0)
    lane = lax.broadcasted_iota(jnp.int32, running.shape, 1)
    shift = 1
    while shift < length:
        running += jnp.where(lane >= shift, pltpu.roll(running, shift, 1), 0.0)
        shift *= 2
    running_ref[...] = running
    column = running.T
    copies[1].wait()
    copies[2].wait()
    for h in range(heads):
        cols = slice(128 * h, 128 * h + 128)
        total = column[length - 1 : length, h : h + 1]
        weight = jnp.exp(total - column[:, h : h + 1])
        high, low = split(k_ref[:, cols].astype(F32) * weight)
        values = v_ref[:, cols]
        state = dot(high, values, TN) + dot(low, values, TN)
        chunks_ref[8 * h : 8 * h + 8, 0:16, :] = state.reshape(8, 16, 128)
        chunks_ref[8 * h : 8 * h + 8, 16:24, :] = jnp.broadcast_to(total.reshape(1, 1, 1), (8, 8, 128))


def prefix_kernel(parent_ref, all_ref, out_ref):
    segments = all_ref.shape[0]
    for s in range(segments):
        first = parent_ref[s]
        p = jnp.clip(first, 0, segments - 1)
        second = parent_ref[p]
        g = jnp.clip(second, 0, segments - 1)
        own = all_ref[p, 0:16, :]
        factor = jnp.exp(all_ref[p, 16:24, :])
        factor = jnp.concatenate([factor, factor], axis=0)
        older = jnp.where(second >= 0, factor * all_ref[g, 0:16, :], 0.0)
        out_ref[s] = jnp.where(first >= 0, own + older, 0.0)


def within_kernel(first, q_hbm, k_hbm, v_hbm, running_ref, out_ref, *rest):
    q_ref, k_ref, v_ref, sems = rest[-4:]
    copies = load(sems, (q_hbm, q_ref), (k_hbm, k_ref), (v_hbm, v_ref))
    length = q_ref.shape[0]
    size = 256
    scale = 128 ** (-0.5)
    causal = lax.broadcasted_iota(jnp.int32, (size, size), 0) >= lax.broadcasted_iota(jnp.int32, (size, size), 1)
    column = running_ref[...].T
    for copy in copies:
        copy.wait()
    for h in range(first, first + 2):
        cols = slice(128 * h, 128 * h + 128)
        for i in range(length // size):
            rows = slice(size * i, size * i + size)
            q = q_ref[rows, cols]
            total = None
            for j in range(i + 1):
                inner = slice(size * j, size * j + size)
                scores = dot(q, k_ref[inner, cols], NT)
                gap = column[rows, h : h + 1] - running_ref[h : h + 1, inner]
                factor = jnp.exp(jnp.minimum(gap, 0.0))
                if i == j:
                    factor = jnp.where(causal, factor, 0.0)
                weights = (scores * scale * factor).astype(BF16)
                term = dot(weights, v_ref[inner, cols])
                total = term if total is None else total + term
            out_ref[rows, cols.start - 128 * first : cols.stop - 128 * first] = total
    if len(rest) > 4:
        rest[0][...] = q_ref[...]


def mix_kernel(q_ref, prefix_ref, early_ref, late_ref, running_ref, gain_ref, out_ref, squares_ref):
    parts, share = out_ref.shape[:2]
    growth = jnp.exp(running_ref[...].T)
    squares = None
    for h in range(4):
        cols = slice(128 * h, 128 * h + 128)
        high, low = split(prefix_ref[h])
        q = q_ref[:, cols]
        inner = (early_ref if h < 2 else late_ref)[:, 128 * (h % 2) : 128 * (h % 2) + 128]
        attention = (dot(q, high) + dot(q, low)) * growth[:, h : h + 1] + inner
        term = jnp.sum(attention * attention, axis=1, keepdims=True)
        squares = term if squares is None else squares + term
        out_ref[:, :, cols] = (attention * gain_ref[:, cols]).astype(BF16).reshape(parts, share, 128)
    squares_ref[...] = jnp.broadcast_to(squares, (parts * share, 128)).reshape(parts, share, 128)


def project_kernel(step, start, index_ref, features_ref, squares_ref, w_hbm, keep_ref, send_ref, w_ref, sems):
    own, other = index_ref[2 * step], index_ref[2 * step + 1]
    rows = features_ref.shape[1]
    width = keep_ref.shape[1] - (128 if start == 0 else 0)
    tiles = [slice(n, n + 512) for n in range(0, width, 512)]
    copies = load(sems, *[(w_hbm.at[:, start + t.start : start + t.stop], w_ref.at[:, t]) for t in tiles])
    left = jnp.concatenate([features_ref[own], features_ref[other]], axis=0)
    for copy, t in zip(copies, tiles):
        copy.wait()
        both = dot(left, w_ref[:, t])
        keep_ref[:, t] = both[:rows]
        send_ref[:, t] = both[rows:]
    if start == 0:
        keep_ref[:, width:] = squares_ref[own]
        send_ref[:, width:] = squares_ref[other]


def add_kernel(index_ref, keep_ref, arrived_ref, total_ref, next_ref):
    total_ref[...] = keep_ref[...] + arrived_ref[...]
    for i in range(8):
        next_ref[i] = index_ref[i]


def finish_kernel(start, features, *refs):
    terms = refs[:3]
    if start == 0:
        out_hbm, inverse_ref, buffer, sems = refs[3:]
        width = terms[0].shape[1] - 128
        squares = terms[0][:, width:] + terms[1][:, width:] + terms[2][:, width:]
        inverse_ref[...] = 1.0 / jnp.sqrt(squares / features + 1e-06)
    else:
        inverse_ref, _, out_hbm, buffer, sems = refs[3:]
        width = terms[0].shape[1]
    inverse = inverse_ref[:, 0:1]
    tile = 1024
    copies = []
    for i, n in enumerate(range(0, width, tile)):
        cols = slice(n, n + tile)
        buffer[:, cols] = ((terms[0][:, cols] + terms[1][:, cols] + terms[2][:, cols]) * inverse).astype(BF16)
        copy = pltpu.make_async_copy(buffer.at[:, cols], out_hbm.at[:, start + n : start + n + tile], sems.at[i])
        copy.start()
        copies.append(copy)
    for copy in copies:
        copy.wait()


VMEM = pl.BlockSpec(memory_space=pltpu.VMEM)
SMEM = pl.BlockSpec(memory_space=pltpu.SMEM)
ANY = pl.BlockSpec(memory_space=pl.ANY)
HBM = pl.BlockSpec(memory_space=pltpu.HBM)


def call(kernel, shapes, ins, outs=None, scratch=(), aliases=None, flops=2**28, moved=2**20, vmem=16 * 2**20):
    return pl.pallas_call(
        kernel,
        out_shape=[jax.ShapeDtypeStruct(s, d) for s, d in shapes],
        in_specs=ins,
        out_specs=outs or [VMEM] * len(shapes),
        scratch_shapes=list(scratch),
        input_output_aliases=aliases or {},
        compiler_params=pltpu.CompilerParams(vmem_limit_bytes=vmem),
        cost_estimate=pl.CostEstimate(flops=flops, bytes_accessed=moved, transcendentals=0),
    )


def head_pairs(target):
    pairs = []
    for y in range(4):
        for core in range(2):
            to, to_core = target(y, core)
            pairs.append((2 * y + core, 2 * (to % 4) + to_core))
    return pairs


SWAP = head_pairs(lambda y, core: (y, 1 - core))
RING = head_pairs(lambda y, core: (y + 1 - 2 * core, core))

def per_device(q, k, v, log_decay, parent, gain, w):
    length, width = q.shape
    dma = pltpu.SemaphoreType.DMA
    chunks, running = call(
        state_kernel,
        [((32, 24, 128), F32), ((8, length), F32)],
        [HBM] * 3,
        scratch=[pltpu.VMEM(log_decay.shape, F32), pltpu.VMEM(k.shape, BF16), pltpu.VMEM(v.shape, BF16), dma((3,))],
        vmem=253 * 2**18,
    )(log_decay, k, v)
    everyone = lax.all_to_all(chunks, "seg", 0, 0, tiled=True)
    inputs = [pltpu.VMEM(q.shape, BF16)] * 3 + [dma((3,))]
    (early,) = call(
        functools.partial(within_kernel, 0), [((length, width // 2), F32)], [HBM] * 3 + [VMEM], scratch=inputs, flops=2**30
    )(q, k, v, running)
    everyone, early, running = lax.optimization_barrier((everyone, early, running))
    (mine,) = call(prefix_kernel, [((32, 16, 128), F32)], [SMEM, VMEM])(parent, everyone)
    prefix = lax.all_to_all(mine, "seg", 0, 0, tiled=True).reshape(4, 128, 128)
    late, q_near = call(
        functools.partial(within_kernel, 2),
        [((length, width // 2), F32), (q.shape, BF16)],
        [HBM] * 3 + [VMEM],
        scratch=inputs,
        flops=2**30,
    )(q, k, v, running)
    me = lax.axis_index("head")
    y, core = me >> 1, me & 1
    way = (1 - 2 * core) * jnp.arange(1, 5, dtype=jnp.int32)
    blocks = jnp.stack([((y - way) & 3) * 2 + core, ((y + way) & 3) * 2 + 1 - core], axis=1).reshape(8)
    share = length // 8
    features, squares = call(mix_kernel, [((8, share, width), BF16), ((8, share, 128), F32)], [VMEM] * 6)(
        q_near, prefix, early, late, running, gain.reshape(1, width)
    )
    chunks = 2
    part = w.shape[1] // chunks
    arrived = [None] * chunks
    for step in range(1, 5):
        terms = []
        for chunk in range(chunks):
            start = chunk * part
            shape = ((share, part + (128 if chunk == 0 else 0)), F32)
            keep, send = call(
                functools.partial(project_kernel, step - 1, start),
                [shape, shape],
                [SMEM, VMEM, VMEM, HBM],
                scratch=[pltpu.VMEM((width, part), BF16), dma((part // 512,))],
                flops=2**22,
                moved=2**14,
                vmem=(50 if step == 1 else 16) * 2**20,
            )(blocks, features, squares, w)
            terms.append([keep, lax.ppermute(send, "head", SWAP)] + ([arrived[chunk]] if step > 1 else []))
        if step < 4:
            totals = [None] * chunks
            for chunk in reversed(range(chunks)):
                t = terms[chunk]
                if step == 1:
                    totals[chunk], blocks = call(
                        add_kernel, [(t[0].shape, F32), ((8,), jnp.int32)], [SMEM, VMEM, VMEM], outs=[VMEM, SMEM], flops=2**20, moved=2**14
                    )(blocks, *t)
                else:
                    totals[chunk] = sum(t[1:], t[0])
            arrived = [lax.ppermute(total, "head", RING) for total in totals]
    out = ((share, w.shape[1]), BF16)
    scratch = [pltpu.VMEM((share, part), BF16), dma((part // 1024,))]
    total_features = width * lax.axis_size("head")
    half, inverse = call(
        functools.partial(finish_kernel, 0, total_features),
        [out, ((share, 128), F32)],
        [VMEM] * 3,
        outs=[ANY, VMEM],
        scratch=scratch,
    )(*terms[0])
    (mixed,) = call(
        functools.partial(finish_kernel, part, total_features),
        [out],
        [VMEM] * 4 + [ANY],
        outs=[ANY],
        scratch=scratch,
        aliases={4: 0},
    )(*terms[1], inverse, half)
    return mixed


def solution(mesh):
    return jax.shard_map(
        per_device,
        mesh=mesh,
        in_specs=(P("seg", "head"), P("seg", "head"), P("seg", "head"), P("head", "seg"), P(), P("head"), P("head", None)),
        out_specs=P(("seg", "head"), None),
        check_vma=False,
    )
```

```python
import functools
import jax
import jax.numpy as jnp
from jax import lax
from jax.experimental import pallas as pl
from jax.experimental.pallas import tpu as pltpu
from jax.sharding import PartitionSpec as P

F32, BF16 = jnp.float32, jnp.bfloat16
NT = (((1,), (1,)), ((), ()))
TN = (((0,), (0,)), ((), ()))
NN = (((1,), (0,)), ((), ()))


def dot(a, b, dims=NN):
    return lax.dot_general(a, b, dims, preferred_element_type=F32)


def split(x):
    high = x.astype(BF16)
    return high, (x - high.astype(F32)).astype(BF16)


def load(sems, *pairs):
    copies = [pltpu.make_async_copy(source, target, sems.at[i]) for i, (source, target) in enumerate(pairs)]
    for copy in copies:
        copy.start()
    return copies


def state_kernel(decay_hbm, k_hbm, v_hbm, chunks_ref, running_ref, decay_ref, k_ref, v_ref, sems):
    copies = load(sems, (decay_hbm, decay_ref), (k_hbm, k_ref), (v_hbm, v_ref))
    copies[0].wait()
    heads, length = decay_ref.shape
    running = jnp.concatenate([decay_ref[...]] * (8 // heads), axis=0)
    lane = lax.broadcasted_iota(jnp.int32, running.shape, 1)
    shift = 1
    while shift < length:
        running += jnp.where(lane >= shift, pltpu.roll(running, shift, 1), 0.0)
        shift *= 2
    running_ref[...] = running
    column = running.T
    copies[1].wait()
    copies[2].wait()
    for h in range(heads):
        cols = slice(128 * h, 128 * h + 128)
        total = column[length - 1 : length, h : h + 1]
        weight = jnp.exp(total - column[:, h : h + 1])
        high, low = split(k_ref[:, cols].astype(F32) * weight)
        values = v_ref[:, cols]
        state = dot(high, values, TN) + dot(low, values, TN)
        chunks_ref[8 * h : 8 * h + 8, 0:16, :] = state.reshape(8, 16, 128)
        chunks_ref[8 * h : 8 * h + 8, 16:24, :] = jnp.broadcast_to(total.reshape(1, 1, 1), (8, 8, 128))


def prefix_kernel(parent_ref, all_ref, out_ref):
    segments = all_ref.shape[0]
    for s in range(segments):
        first = parent_ref[s]
        p = jnp.clip(first, 0, segments - 1)
        second = parent_ref[p]
        g = jnp.clip(second, 0, segments - 1)
        own = all_ref[p, 0:16, :]
        factor = jnp.exp(all_ref[p, 16:24, :])
        factor = jnp.concatenate([factor, factor], axis=0)
        older = jnp.where(second >= 0, factor * all_ref[g, 0:16, :], 0.0)
        out_ref[s] = jnp.where(first >= 0, own + older, 0.0)


def within_kernel(first, q_hbm, k_hbm, v_hbm, running_ref, out_ref, q_ref, k_ref, v_ref, sems):
    copies = load(sems, (q_hbm, q_ref), (k_hbm, k_ref), (v_hbm, v_ref))
    length = q_ref.shape[0]
    size = 256
    scale = 128 ** (-0.5)
    causal = lax.broadcasted_iota(jnp.int32, (size, size), 0) >= lax.broadcasted_iota(jnp.int32, (size, size), 1)
    column = running_ref[...].T
    for copy in copies:
        copy.wait()
    for h in range(first, first + 2):
        cols = slice(128 * h, 128 * h + 128)
        for i in range(length // size):
            rows = slice(size * i, size * i + size)
            q = q_ref[rows, cols]
            total = None
            for j in range(i + 1):
                inner = slice(size * j, size * j + size)
                scores = dot(q, k_ref[inner, cols], NT)
                gap = column[rows, h : h + 1] - running_ref[h : h + 1, inner]
                factor = jnp.exp(jnp.minimum(gap, 0.0))
                if i == j:
                    factor = jnp.where(causal, factor, 0.0)
                weights = (scores * scale * factor).astype(BF16)
                term = dot(weights, v_ref[inner, cols])
                total = term if total is None else total + term
            out_ref[rows, cols.start - 128 * first : cols.stop - 128 * first] = total


def mix_kernel(
    index_ref, q_hbm, prefix_ref, early_ref, late_ref, running_ref, gain_ref, _,
    out_ref, squares_out_ref,
    features_ref, squares_ref, q_ref, sems,
):
    heads = [slice(128 * h, 128 * h + 128) for h in range(4)]
    inputs = load(sems, *[(q_hbm.at[:, cols], q_ref.at[:, cols]) for cols in heads])
    parts, share, width = out_ref.shape
    growth = jnp.exp(running_ref[...].T)
    squares = None
    for h in range(4):
        cols = slice(128 * h, 128 * h + 128)
        high, low = split(prefix_ref[h])
        inputs[h].wait()
        q = q_ref[:, cols]
        inner = (early_ref if h < 2 else late_ref)[:, 128 * (h % 2) : 128 * (h % 2) + 128]
        attention = (dot(q, high) + dot(q, low)) * growth[:, h : h + 1] + inner
        term = jnp.sum(attention * attention, axis=1, keepdims=True)
        squares = term if squares is None else squares + term
        features_ref[:, :, cols] = (attention * gain_ref[:, cols]).astype(BF16).reshape(parts, share, 128)
    squares_ref[...] = jnp.broadcast_to(squares, (parts * share, 128)).reshape(parts, share, 128)
    for i in range(parts):
        out_ref[i] = features_ref[index_ref[i]]
        squares_out_ref[i] = squares_ref[index_ref[i]]


def project_kernel(start, first, features_ref, squares_ref, w_ref, *refs):
    keep_ref, send_ref = refs[-2:]
    count, rows = keep_ref.shape[:2]
    width = keep_ref.shape[2] - (128 if start == 0 else 0)
    sides = [slice(first, first + count), slice(4 + first, 4 + first + count)]
    left = jnp.concatenate([features_ref[side].reshape(count * rows, -1) for side in sides], axis=0)
    for n in range(0, width, 512):
        t = slice(n, n + 512)
        both = dot(left, w_ref[:, start + n : start + n + 512])
        keep_ref[:, :, t] = both[: count * rows].reshape(count, rows, 512)
        send_ref[:, :, t] = both[count * rows :].reshape(count, rows, 512)
    if start == 0:
        keep_ref[:, :, width:] = squares_ref[sides[0]]
        send_ref[:, :, width:] = squares_ref[sides[1]]


def finish_kernel(start, features, *refs):
    mine_ref, arrived_ref = refs[:2]
    if start == 0:
        out_hbm, inverse_ref, buffer, sems = refs[2:]
        width = mine_ref.shape[1] - 128
        inverse_ref[...] = 1.0 / jnp.sqrt((mine_ref[:, width:] + arrived_ref[:, width:]) / features + 1e-06)
    else:
        inverse_ref, _, out_hbm, buffer, sems = refs[2:]
        width = mine_ref.shape[1]
    inverse = inverse_ref[:, 0:1]
    tile = 512
    copies = []
    for i, n in enumerate(range(0, width, tile)):
        cols = slice(n, n + tile)
        buffer[:, cols] = ((mine_ref[:, cols] + arrived_ref[:, cols]) * inverse).astype(BF16)
        copy = pltpu.make_async_copy(buffer.at[:, cols], out_hbm.at[:, start + n : start + n + tile], sems.at[i])
        copy.start()
        copies.append(copy)
    for copy in copies:
        copy.wait()


VMEM = pl.BlockSpec(memory_space=pltpu.VMEM)
SMEM = pl.BlockSpec(memory_space=pltpu.SMEM)
ANY = pl.BlockSpec(memory_space=pl.ANY)
HBM = pl.BlockSpec(memory_space=pltpu.HBM)


def call(kernel, shapes, ins, outs=None, scratch=(), aliases=None, flops=2**28, moved=2**20, vmem=6 * 2**20):
    return pl.pallas_call(
        kernel,
        out_shape=[jax.ShapeDtypeStruct(s, d) for s, d in shapes],
        in_specs=ins,
        out_specs=outs or [VMEM] * len(shapes),
        scratch_shapes=list(scratch),
        input_output_aliases=aliases or {},
        compiler_params=pltpu.CompilerParams(vmem_limit_bytes=vmem),
        cost_estimate=pl.CostEstimate(flops=flops, bytes_accessed=moved, transcendentals=0),
    )


def head_pairs(target):
    pairs = []
    for y in range(4):
        for core in range(2):
            to, to_core = target(y, core)
            pairs.append((2 * y + core, 2 * (to % 4) + to_core))
    return pairs


SWAP = head_pairs(lambda y, core: (y, 1 - core))
RING = head_pairs(lambda y, core: (y + 1 - 2 * core, core))

def per_device(q, k, v, log_decay, parent, gain, w):
    length, width = q.shape
    dma = pltpu.SemaphoreType.DMA
    chunks, running = call(
        state_kernel,
        [((32, 24, 128), F32), ((8, length), F32)],
        [HBM] * 3,
        scratch=[pltpu.VMEM(log_decay.shape, F32), pltpu.VMEM(k.shape, BF16), pltpu.VMEM(v.shape, BF16), dma((3,))],
        vmem=253 * 2**18,
    )(log_decay, k, v)
    everyone = lax.all_to_all(chunks, "seg", 0, 0, tiled=True)
    inputs = [pltpu.VMEM(q.shape, BF16)] * 3 + [dma((3,))]
    (early,) = call(
        functools.partial(within_kernel, 0), [((length, width // 2), F32)], [HBM] * 3 + [VMEM], scratch=inputs, flops=2**30
    )(q, k, v, running)
    everyone, early, running = lax.optimization_barrier((everyone, early, running))
    (mine,) = call(prefix_kernel, [((32, 16, 128), F32)], [SMEM, VMEM])(parent, everyone)
    prefix = lax.all_to_all(mine, "seg", 0, 0, tiled=True).reshape(4, 128, 128)
    (late,) = call(
        functools.partial(within_kernel, 2), [((length, width // 2), F32)], [HBM] * 3 + [VMEM], scratch=inputs, flops=2**30
    )(q, k, v, running)
    me = lax.axis_index("head")
    y, core = me >> 1, me & 1
    way = (1 - 2 * core) * jnp.arange(1, 5, dtype=jnp.int32)
    blocks = jnp.concatenate([((y - way) & 3) * 2 + core, ((y + way) & 3) * 2 + 1 - core])
    share = length // 8
    starts = [0, 2048, 4096]
    widths = [2048, 2048, 2048]

    features, squares = call(
        mix_kernel,
        [((8, share, width), BF16), ((8, share, 128), F32)],
        [SMEM, HBM, VMEM, VMEM, VMEM, VMEM, VMEM, HBM],
        scratch=[pltpu.VMEM((8, share, width), BF16), pltpu.VMEM((8, share, 128), F32), pltpu.VMEM(q.shape, BF16)]
        + [dma((4,))],
        vmem=50 * 2**20,
    )(blocks, q, prefix, early, late, running, gain.reshape(1, width), w)

    def project(start, size, first, after):
        return call(
            functools.partial(project_kernel, start, first),
            [((1, share, size + (128 if start == 0 else 0)), F32)] * 2,
            [VMEM, VMEM, VMEM] + [ANY] * len(after),

        )(features, squares, w, *after)

    before, arrived = [], []
    for step in range(4):
        totals = []
        for i, (start, size) in enumerate(zip(starts, widths)):
            keep, send = project(start, size, step, before if step == 1 else before[i : i + 1] if step > 1 else [])
            totals.append(keep[0] + lax.ppermute(send[0], "head", SWAP) + (arrived[i] if step in (1, 2) else 0.0))
        if step < 3:
            before = totals if step == 0 else arrived
            arrived = [lax.ppermute(total, "head", RING) for total in totals]
    total_features = width * lax.axis_size("head")
    out = ((share, w.shape[1]), BF16)
    mixed = None
    for start, size, own, got in zip(starts, widths, totals, arrived):
        buffers = [pltpu.VMEM((share, size), BF16), dma((size // 512,))]
        kernel = functools.partial(finish_kernel, start, total_features)
        if start == 0:
            mixed, inverse = call(kernel, [out, ((share, 128), F32)], [VMEM] * 2, outs=[ANY, VMEM], scratch=buffers)(own, got)
        else:
            (mixed,) = call(kernel, [out], [VMEM] * 3 + [ANY], outs=[ANY], scratch=buffers, aliases={3: 0})(
                own, got, inverse, mixed
            )
    return mixed


def solution(mesh):
    return jax.shard_map(
        per_device,
        mesh=mesh,
        in_specs=(P("seg", "head"), P("seg", "head"), P("seg", "head"), P("head", "seg"), P(), P("head"), P("head", None)),
        out_specs=P(("seg", "head"), None),
        check_vma=False,
    )
```

```python
import functools
import jax
import jax.numpy as jnp
from jax import lax
from jax.experimental import pallas as pl
from jax.experimental.pallas import tpu as pltpu
from jax.sharding import PartitionSpec as P

F32, BF16 = jnp.float32, jnp.bfloat16
NT = (((1,), (1,)), ((), ()))
TN = (((0,), (0,)), ((), ()))
NN = (((1,), (0,)), ((), ()))


def dot(a, b, dims=NN):
    return lax.dot_general(a, b, dims, preferred_element_type=F32)


def split(x):
    high = x.astype(BF16)
    return high, (x - high.astype(F32)).astype(BF16)


def load(sems, *pairs):
    copies = [pltpu.make_async_copy(source, target, sems.at[i]) for i, (source, target) in enumerate(pairs)]
    for copy in copies:
        copy.start()
    return copies


def state_kernel(decay_hbm, k_hbm, v_hbm, chunks_ref, running_ref, decay_ref, k_ref, v_ref, sems):
    copies = load(sems, (decay_hbm, decay_ref), (k_hbm, k_ref), (v_hbm, v_ref))
    copies[0].wait()
    heads, length = decay_ref.shape
    running = jnp.concatenate([decay_ref[...]] * (8 // heads), axis=0)
    lane = lax.broadcasted_iota(jnp.int32, running.shape, 1)
    shift = 1
    while shift < length:
        running += jnp.where(lane >= shift, pltpu.roll(running, shift, 1), 0.0)
        shift *= 2
    running_ref[...] = running
    column = running.T
    copies[1].wait()
    copies[2].wait()
    for h in range(heads):
        cols = slice(128 * h, 128 * h + 128)
        total = column[length - 1 : length, h : h + 1]
        weight = jnp.exp(total - column[:, h : h + 1])
        high, low = split(k_ref[:, cols].astype(F32) * weight)
        values = v_ref[:, cols]
        state = dot(high, values, TN) + dot(low, values, TN)
        chunks_ref[8 * h : 8 * h + 8, 0:16, 0, :] = state.reshape(8, 16, 128)
        chunks_ref[8 * h : 8 * h + 8, 16, 0, :] = jnp.broadcast_to(total, (8, 128))


def prefix_kernel(parent_ref, all_ref, out_ref):
    segments = all_ref.shape[0]
    for s in range(segments):
        first = parent_ref[s]
        p = jnp.clip(first, 0, segments - 1)
        second = parent_ref[p]
        g = jnp.clip(second, 0, segments - 1)
        own = all_ref[p, 0:16, 0, :]
        factor = jnp.exp(all_ref[p, 16:17, 0, :])
        older = jnp.where(second >= 0, factor * all_ref[g, 0:16, 0, :], 0.0)
        out_ref[s] = jnp.where(first >= 0, own + older, 0.0)


def within_kernel(first, q_hbm, k_hbm, v_hbm, running_ref, out_ref, q_ref, k_ref, v_ref, sems):
    copies = load(sems, (q_hbm, q_ref), (k_hbm, k_ref), (v_hbm, v_ref))
    length = q_ref.shape[0]
    size = 256
    scale = 128 ** (-0.5)
    causal = lax.broadcasted_iota(jnp.int32, (size, size), 0) >= lax.broadcasted_iota(jnp.int32, (size, size), 1)
    column = running_ref[...].T
    for copy in copies:
        copy.wait()
    for h in range(first, first + 2):
        cols = slice(128 * h, 128 * h + 128)
        for i in range(length // size):
            rows = slice(size * i, size * i + size)
            q = q_ref[rows, cols]
            total = None
            for j in range(i + 1):
                inner = slice(size * j, size * j + size)
                scores = dot(q, k_ref[inner, cols], NT)
                gap = column[rows, h : h + 1] - running_ref[h : h + 1, inner]
                factor = jnp.exp(jnp.minimum(gap, 0.0))
                if i == j:
                    factor = jnp.where(causal, factor, 0.0)
                weights = (scores * scale * factor).astype(BF16)
                term = dot(weights, v_ref[inner, cols])
                total = term if total is None else total + term
            out_ref[rows, cols.start - 128 * first : cols.stop - 128 * first] = total


def mix_kernel(
    index_ref, q_hbm, prefix_ref, early_ref, late_ref, running_ref, gain_ref, _,
    out_ref, squares_out_ref,
    features_ref, squares_ref, q_ref, sems,
):
    heads = [slice(128 * h, 128 * h + 128) for h in range(4)]
    inputs = load(sems, *[(q_hbm.at[:, cols], q_ref.at[:, cols]) for cols in heads])
    parts, share, width = out_ref.shape
    growth = jnp.exp(running_ref[...].T)
    squares = None
    for h in range(4):
        cols = slice(128 * h, 128 * h + 128)
        high, low = split(prefix_ref[h])
        inputs[h].wait()
        q = q_ref[:, cols]
        inner = (early_ref if h < 2 else late_ref)[:, 128 * (h % 2) : 128 * (h % 2) + 128]
        attention = (dot(q, high) + dot(q, low)) * growth[:, h : h + 1] + inner
        term = jnp.sum(attention * attention, axis=1, keepdims=True)
        squares = term if squares is None else squares + term
        features_ref[:, :, cols] = (attention * gain_ref[:, cols]).astype(BF16).reshape(parts, share, 128)
    squares_ref[...] = jnp.broadcast_to(squares, (parts * share, 128)).reshape(parts, share, 128)
    for i in range(parts):
        out_ref[i] = features_ref[index_ref[i]]
        squares_out_ref[i] = squares_ref[index_ref[i]]


def project_kernel(start, size, first, features_ref, squares_ref, w_ref, *refs):
    keep_ref, send_ref = refs[-2:]
    count, rows = keep_ref.shape[:2]
    sides = [slice(first, first + count), slice(4 + first, 4 + first + count)]
    left = jnp.concatenate([features_ref[side].reshape(count * rows, -1) for side in sides], axis=0)
    for n in range(0, size, 512):
        t = slice(n, n + 512)
        both = dot(left, w_ref[:, start + n : start + n + 512])
        keep_ref[:, :, t] = both[: count * rows].reshape(count, rows, 512)
        send_ref[:, :, t] = both[count * rows :].reshape(count, rows, 512)
    if keep_ref.shape[2] > size:
        keep_ref[:, :, size:] = squares_ref[sides[0]]
        send_ref[:, :, size:] = squares_ref[sides[1]]


def finish_kernel(start, extra, features, *refs):
    mine_ref, arrived_ref = refs[:2]
    if extra:
        out_hbm, inverse_ref, buffer, sems = refs[2:]
        width = mine_ref.shape[1] - extra
        inverse_ref[...] = 1.0 / jnp.sqrt((mine_ref[:, width:] + arrived_ref[:, width:]) / features + 1e-06)
    else:
        inverse_ref, _, out_hbm, buffer, sems = refs[2:]
        width = mine_ref.shape[1]
    inverse = inverse_ref[:, 0:1]
    tile = 512
    copies = []
    for i, n in enumerate(range(0, width, tile)):
        cols = slice(n, n + tile)
        buffer[:, cols] = ((mine_ref[:, cols] + arrived_ref[:, cols]) * inverse).astype(BF16)
        copy = pltpu.make_async_copy(buffer.at[:, cols], out_hbm.at[:, start + n : start + n + tile], sems.at[i])
        copy.start()
        copies.append(copy)
    for copy in copies:
        copy.wait()


VMEM = pl.BlockSpec(memory_space=pltpu.VMEM)
SMEM = pl.BlockSpec(memory_space=pltpu.SMEM)
ANY = pl.BlockSpec(memory_space=pl.ANY)
HBM = pl.BlockSpec(memory_space=pltpu.HBM)


def call(kernel, shapes, ins, outs=None, scratch=(), aliases=None, flops=2**28, moved=2**20, vmem=6 * 2**20):
    return pl.pallas_call(
        kernel,
        out_shape=[jax.ShapeDtypeStruct(s, d) for s, d in shapes],
        in_specs=ins,
        out_specs=outs or [VMEM] * len(shapes),
        scratch_shapes=list(scratch),
        input_output_aliases=aliases or {},
        compiler_params=pltpu.CompilerParams(vmem_limit_bytes=vmem),
        cost_estimate=pl.CostEstimate(flops=flops, bytes_accessed=moved, transcendentals=0),
    )


def head_pairs(target):
    pairs = []
    for y in range(4):
        for core in range(2):
            to, to_core = target(y, core)
            pairs.append((2 * y + core, 2 * (to % 4) + to_core))
    return pairs


SWAP = head_pairs(lambda y, core: (y, 1 - core))
RING = head_pairs(lambda y, core: (y + 1 - 2 * core, core))

def per_device(q, k, v, log_decay, parent, gain, w):
    length, width = q.shape
    dma = pltpu.SemaphoreType.DMA
    chunks, running = call(
        state_kernel,
        [((32, 17, 1, 128), F32), ((8, length), F32)],
        [HBM] * 3,
        scratch=[pltpu.VMEM(log_decay.shape, F32), pltpu.VMEM(k.shape, BF16), pltpu.VMEM(v.shape, BF16), dma((3,))],
        vmem=253 * 2**18,
    )(log_decay, k, v)
    everyone = lax.all_to_all(chunks, "seg", 0, 0, tiled=True)
    inputs = [pltpu.VMEM(q.shape, BF16)] * 3 + [dma((3,))]
    (early,) = call(
        functools.partial(within_kernel, 0), [((length, width // 2), F32)], [HBM] * 3 + [VMEM], scratch=inputs, flops=2**30
    )(q, k, v, running)
    everyone, early, running = lax.optimization_barrier((everyone, early, running))
    (mine,) = call(prefix_kernel, [((32, 16, 128), F32)], [SMEM, VMEM])(parent, everyone)
    prefix = lax.all_to_all(mine, "seg", 0, 0, tiled=True).reshape(4, 128, 128)
    (late,) = call(
        functools.partial(within_kernel, 2), [((length, width // 2), F32)], [HBM] * 3 + [VMEM], scratch=inputs, flops=2**30
    )(q, k, v, running)
    me = lax.axis_index("head")
    y, core = me >> 1, me & 1
    way = (1 - 2 * core) * jnp.arange(1, 5, dtype=jnp.int32)
    blocks = jnp.concatenate([((y - way) & 3) * 2 + core, ((y + way) & 3) * 2 + 1 - core])
    share = length // 8
    starts = [0, 1536, 3584]
    widths = [1536, 2048, 2560]
    extras = [128, 0, 0]

    features, squares = call(
        mix_kernel,
        [((8, share, width), BF16), ((8, share, 128), F32)],
        [SMEM, HBM, VMEM, VMEM, VMEM, VMEM, VMEM, HBM],
        scratch=[pltpu.VMEM((8, share, width), BF16), pltpu.VMEM((8, share, 128), F32), pltpu.VMEM(q.shape, BF16)]
        + [dma((4,))],
        vmem=50 * 2**20,
    )(blocks, q, prefix, early, late, running, gain.reshape(1, width), w)

    def project(start, size, extra, first, after):
        return call(
            functools.partial(project_kernel, start, size, first),
            [((1, share, size + extra), F32)] * 2,
            [VMEM, VMEM, VMEM] + [ANY] * len(after),

        )(features, squares, w, *after)

    before, arrived = [], []
    for step in range(4):
        totals = []
        for i, (start, size, extra) in enumerate(zip(starts, widths, extras)):
            keep, send = project(start, size, extra, step, before if step == 1 else before[i : i + 1] if step > 1 else [])
            totals.append(keep[0] + lax.ppermute(send[0], "head", SWAP) + (arrived[i] if step in (1, 2) else 0.0))
        if step < 3:
            before = totals if step == 0 else arrived
            arrived = [lax.ppermute(total, "head", RING) for total in totals]
    total_features = width * lax.axis_size("head")
    out = ((share, w.shape[1]), BF16)
    for extra, start, size, i in sorted(zip(extras, starts, widths, range(len(starts))), key=lambda c: -c[0]):
        buffers = [pltpu.VMEM((share, size), BF16), dma((size // 512,))]
        kernel = functools.partial(finish_kernel, start, extra, total_features)
        terms = [totals[i], arrived[i]]
        if extra:
            mixed, inverse = call(kernel, [out, ((share, 128), F32)], [VMEM] * 2, outs=[ANY, VMEM], scratch=buffers)(*terms)
        else:
            (mixed,) = call(kernel, [out], [VMEM] * 3 + [ANY], outs=[ANY], scratch=buffers, aliases={3: 0})(
                *terms, inverse, mixed
            )
    return mixed


def solution(mesh):
    return jax.shard_map(
        per_device,
        mesh=mesh,
        in_specs=(P("seg", "head"), P("seg", "head"), P("seg", "head"), P("head", "seg"), P(), P("head"), P("head", None)),
        out_specs=P(("seg", "head"), None),
        check_vma=False,
    )
```

```python
import functools
import jax
import jax.numpy as jnp
from jax import lax
from jax.experimental import pallas as pl
from jax.experimental.pallas import tpu as pltpu
from jax.sharding import PartitionSpec as P

F32, BF16 = jnp.float32, jnp.bfloat16
NT = (((1,), (1,)), ((), ()))
TN = (((0,), (0,)), ((), ()))
NN = (((1,), (0,)), ((), ()))


def dot(a, b, dims=NN):
    return lax.dot_general(a, b, dims, preferred_element_type=F32)


def split(x):
    high = x.astype(BF16)
    return high, (x - high.astype(F32)).astype(BF16)


def load(sems, *pairs):
    copies = [pltpu.make_async_copy(source, target, sems.at[i]) for i, (source, target) in enumerate(pairs)]
    for copy in copies:
        copy.start()
    return copies


def state_kernel(decay_hbm, k_hbm, v_hbm, chunks_ref, running_ref, decay_ref, k_ref, v_ref, sems):
    blocks = [slice(128 * h, 128 * h + 128) for h in range(decay_ref.shape[0])]
    pairs = [(decay_hbm, decay_ref)]
    for cols in blocks:
        pairs += [(k_hbm.at[:, cols], k_ref.at[:, cols]), (v_hbm.at[:, cols], v_ref.at[:, cols])]
    copies = load(sems, *pairs)
    copies[0].wait()
    heads, length = decay_ref.shape
    running = jnp.concatenate([decay_ref[...]] * (8 // heads), axis=0)
    lane = lax.broadcasted_iota(jnp.int32, running.shape, 1)
    shift = 1
    while shift < length:
        running += jnp.where(lane >= shift, pltpu.roll(running, shift, 1), 0.0)
        shift *= 2
    running_ref[...] = running
    for h, cols in enumerate(blocks):
        total = running[h : h + 1, length - 1 : length]
        weight = jnp.exp(total - running[h : h + 1, :])
        copies[1 + 2 * h].wait()
        high, low = split(k_ref[:, cols].T.astype(F32) * weight)
        copies[2 + 2 * h].wait()
        both = dot(jnp.concatenate([high, low], axis=0), v_ref[:, cols])
        state = both[:128] + both[128:]
        chunks_ref[8 * h : 8 * h + 8, 0:16, 0, :] = state.reshape(8, 16, 128)
        chunks_ref[8 * h : 8 * h + 8, 16, 0, :] = jnp.broadcast_to(total, (8, 128))


def prefix_kernel(parent_ref, all_ref, out_ref):
    segments = all_ref.shape[0]
    for s in range(segments):
        first = parent_ref[s]
        p = jnp.clip(first, 0, segments - 1)
        second = parent_ref[p]
        g = jnp.clip(second, 0, segments - 1)
        own = all_ref[p, 0:16, 0, :]
        factor = jnp.exp(all_ref[p, 16:17, 0, :])
        older = jnp.where(second >= 0, factor * all_ref[g, 0:16, 0, :], 0.0)
        out_ref[s] = jnp.where(first >= 0, own + older, 0.0)


def within_kernel(first, q_hbm, k_hbm, v_hbm, running_ref, out_ref, q_ref, k_ref, v_ref, sems):
    copies = load(sems, (q_hbm, q_ref), (k_hbm, k_ref), (v_hbm, v_ref))
    length = q_ref.shape[0]
    size = 256
    scale = 128 ** (-0.5)
    causal = lax.broadcasted_iota(jnp.int32, (size, size), 0) >= lax.broadcasted_iota(jnp.int32, (size, size), 1)
    column = running_ref[...].T
    for copy in copies:
        copy.wait()
    for h in range(first, first + 2):
        cols = slice(128 * h, 128 * h + 128)
        for i in range(length // size):
            rows = slice(size * i, size * i + size)
            q = q_ref[rows, cols]
            total = None
            for j in range(i + 1):
                inner = slice(size * j, size * j + size)
                scores = dot(q, k_ref[inner, cols], NT)
                gap = column[rows, h : h + 1] - running_ref[h : h + 1, inner]
                factor = jnp.exp(jnp.minimum(gap, 0.0))
                if i == j:
                    factor = jnp.where(causal, factor, 0.0)
                weights = (scores * scale * factor).astype(BF16)
                term = dot(weights, v_ref[inner, cols])
                total = term if total is None else total + term
            out_ref[rows, cols.start - 128 * first : cols.stop - 128 * first] = total


def mix_kernel(
    index_ref, q_hbm, prefix_ref, early_ref, late_ref, running_ref, gain_ref, _,
    out_ref, squares_out_ref,
    features_ref, squares_ref, q_ref, sems,
):
    heads = [slice(128 * h, 128 * h + 128) for h in range(4)]
    inputs = load(sems, *[(q_hbm.at[:, cols], q_ref.at[:, cols]) for cols in heads])
    parts, share, width = out_ref.shape
    growth = jnp.exp(running_ref[...].T)
    squares = None
    for h in range(4):
        cols = slice(128 * h, 128 * h + 128)
        high, low = split(prefix_ref[h])
        inputs[h].wait()
        q = q_ref[:, cols]
        inner = (early_ref if h < 2 else late_ref)[:, 128 * (h % 2) : 128 * (h % 2) + 128]
        both = dot(q, jnp.concatenate([high, low], axis=1))
        attention = (both[:, :128] + both[:, 128:]) * growth[:, h : h + 1] + inner
        term = jnp.sum(attention * attention, axis=1, keepdims=True)
        squares = term if squares is None else squares + term
        features_ref[:, :, cols] = (attention * gain_ref[:, cols]).astype(BF16).reshape(parts, share, 128)
    squares_ref[...] = jnp.broadcast_to(squares, (parts * share, 128)).reshape(parts, share, 128)
    for i in range(parts):
        out_ref[i] = features_ref[index_ref[i]]
        squares_out_ref[i] = squares_ref[index_ref[i]]


def project_kernel(start, size, first, features_ref, squares_ref, w_ref, *refs):
    keep_ref, send_ref = refs[-2:]
    count, rows = keep_ref.shape[:2]
    sides = [slice(first, first + count), slice(4 + first, 4 + first + count)]
    left = jnp.concatenate([features_ref[side].reshape(count * rows, -1) for side in sides], axis=0)
    for n in range(0, size, 512):
        t = slice(n, n + 512)
        both = dot(left, w_ref[:, start + n : start + n + 512])
        keep_ref[:, :, t] = both[: count * rows].reshape(count, rows, 512)
        send_ref[:, :, t] = both[count * rows :].reshape(count, rows, 512)
    if keep_ref.shape[2] > size:
        keep_ref[:, :, size:] = squares_ref[sides[0]]
        send_ref[:, :, size:] = squares_ref[sides[1]]


def finish_kernel(start, extra, features, *refs):
    mine_ref, arrived_ref = refs[:2]
    if extra:
        out_hbm, inverse_ref, buffer, sems = refs[2:]
        width = mine_ref.shape[1] - extra
        inverse_ref[...] = 1.0 / jnp.sqrt((mine_ref[:, width:] + arrived_ref[:, width:]) / features + 1e-06)
    else:
        inverse_ref, _, out_hbm, buffer, sems = refs[2:]
        width = mine_ref.shape[1]
    inverse = inverse_ref[:, 0:1]
    tile = 512
    copies = []
    for i, n in enumerate(range(0, width, tile)):
        cols = slice(n, n + tile)
        buffer[:, cols] = ((mine_ref[:, cols] + arrived_ref[:, cols]) * inverse).astype(BF16)
        copy = pltpu.make_async_copy(buffer.at[:, cols], out_hbm.at[:, start + n : start + n + tile], sems.at[i])
        copy.start()
        copies.append(copy)
    for copy in copies:
        copy.wait()


VMEM = pl.BlockSpec(memory_space=pltpu.VMEM)
SMEM = pl.BlockSpec(memory_space=pltpu.SMEM)
ANY = pl.BlockSpec(memory_space=pl.ANY)
HBM = pl.BlockSpec(memory_space=pltpu.HBM)


def call(kernel, shapes, ins, outs=None, scratch=(), aliases=None, flops=2**28, moved=2**20, vmem=6 * 2**20):
    return pl.pallas_call(
        kernel,
        out_shape=[jax.ShapeDtypeStruct(s, d) for s, d in shapes],
        in_specs=ins,
        out_specs=outs or [VMEM] * len(shapes),
        scratch_shapes=list(scratch),
        input_output_aliases=aliases or {},
        compiler_params=pltpu.CompilerParams(vmem_limit_bytes=vmem),
        cost_estimate=pl.CostEstimate(flops=flops, bytes_accessed=moved, transcendentals=0),
    )


def head_pairs(target):
    pairs = []
    for y in range(4):
        for core in range(2):
            to, to_core = target(y, core)
            pairs.append((2 * y + core, 2 * (to % 4) + to_core))
    return pairs


SWAP = head_pairs(lambda y, core: (y, 1 - core))
RING = head_pairs(lambda y, core: (y + 1 - 2 * core, core))

def per_device(q, k, v, log_decay, parent, gain, w):
    length, width = q.shape
    dma = pltpu.SemaphoreType.DMA
    chunks, running = call(
        state_kernel,
        [((32, 17, 1, 128), F32), ((8, length), F32)],
        [HBM] * 3,
        scratch=[pltpu.VMEM(log_decay.shape, F32), pltpu.VMEM(k.shape, BF16), pltpu.VMEM(v.shape, BF16), dma((9,))],
        vmem=253 * 2**18,
    )(log_decay, k, v)
    everyone = lax.all_to_all(chunks, "seg", 0, 0, tiled=True)
    inputs = [pltpu.VMEM(q.shape, BF16)] * 3 + [dma((3,))]
    (early,) = call(
        functools.partial(within_kernel, 0), [((length, width // 2), F32)], [HBM] * 3 + [VMEM], scratch=inputs, flops=2**30
    )(q, k, v, running)
    everyone, early, running = lax.optimization_barrier((everyone, early, running))
    (mine,) = call(prefix_kernel, [((32, 16, 128), F32)], [SMEM, VMEM])(parent, everyone)
    prefix = lax.all_to_all(mine, "seg", 0, 0, tiled=True).reshape(4, 128, 128)
    (late,) = call(
        functools.partial(within_kernel, 2), [((length, width // 2), F32)], [HBM] * 3 + [VMEM], scratch=inputs, flops=2**30, vmem=6*2**20
    )(q, k, v, running)
    me = lax.axis_index("head")
    y, core = me >> 1, me & 1
    way = (1 - 2 * core) * jnp.arange(1, 5, dtype=jnp.int32)
    blocks = jnp.concatenate([((y - way) & 3) * 2 + core, ((y + way) & 3) * 2 + 1 - core])
    share = length // 8
    starts = [0, 1536, 3584]
    widths = [1536, 2048, 2560]
    extras = [128, 0, 0]

    features, squares = call(
        mix_kernel,
        [((8, share, width), BF16), ((8, share, 128), F32)],
        [SMEM, HBM, VMEM, VMEM, VMEM, VMEM, VMEM, HBM],
        scratch=[pltpu.VMEM((8, share, width), BF16), pltpu.VMEM((8, share, 128), F32), pltpu.VMEM(q.shape, BF16)]
        + [dma((4,))],
        vmem=50 * 2**20,
    )(blocks, q, prefix, early, late, running, gain.reshape(1, width), w)

    def project(start, size, extra, first, after):
        return call(
            functools.partial(project_kernel, start, size, first),
            [((1, share, size + extra), F32)] * 2,
            [VMEM, VMEM, VMEM] + [ANY] * len(after),

        )(features, squares, w, *after)

    before, arrived = [], []
    for step in range(4):
        totals = []
        for i, (start, size, extra) in enumerate(zip(starts, widths, extras)):
            keep, send = project(start, size, extra, step, before if step == 1 else before[i : i + 1] if step > 1 else [])
            totals.append(keep[0] + lax.ppermute(send[0], "head", SWAP) + (arrived[i] if step in (1, 2) else 0.0))
        if step < 3:
            before = totals if step == 0 else arrived
            arrived = [lax.ppermute(total, "head", RING) for total in totals]
    total_features = width * lax.axis_size("head")
    out = ((share, w.shape[1]), BF16)
    for extra, start, size, i in sorted(zip(extras, starts, widths, range(len(starts))), key=lambda c: -c[0]):
        buffers = [pltpu.VMEM((share, size), BF16), dma((size // 512,))]
        kernel = functools.partial(finish_kernel, start, extra, total_features)
        terms = [totals[i], arrived[i]]
        if extra:
            mixed, inverse = call(kernel, [out, ((share, 128), F32)], [VMEM] * 2, outs=[ANY, VMEM], scratch=buffers)(*terms)
        else:
            (mixed,) = call(kernel, [out], [VMEM] * 3 + [ANY], outs=[ANY], scratch=buffers, aliases={3: 0})(
                *terms, inverse, mixed
            )
    return mixed


def solution(mesh):
    return jax.shard_map(
        per_device,
        mesh=mesh,
        in_specs=(P("seg", "head"), P("seg", "head"), P("seg", "head"), P("head", "seg"), P(), P("head"), P("head", None)),
        out_specs=P(("seg", "head"), None),
        check_vma=False,
    )
```

```python
import functools
import jax
import jax.numpy as jnp
from jax import lax
from jax.experimental import pallas as pl
from jax.experimental.pallas import tpu as pltpu
from jax.sharding import PartitionSpec as P

F32, BF16 = jnp.float32, jnp.bfloat16
NT = (((1,), (1,)), ((), ()))
TN = (((0,), (0,)), ((), ()))
NN = (((1,), (0,)), ((), ()))


def dot(a, b, dims=NN):
    return lax.dot_general(a, b, dims, preferred_element_type=F32)


def split(x):
    high = x.astype(BF16)
    return high, (x - high.astype(F32)).astype(BF16)


def load(sems, *pairs):
    copies = [pltpu.make_async_copy(source, target, sems.at[i]) for i, (source, target) in enumerate(pairs)]
    for copy in copies:
        copy.start()
    return copies


def state_kernel(decay_hbm, k_hbm, v_hbm, chunks_ref, running_ref, decay_ref, k_ref, v_ref, sems):
    copies = load(sems, (decay_hbm, decay_ref), (k_hbm, k_ref), (v_hbm, v_ref))
    copies[0].wait()
    heads, length = decay_ref.shape
    running = jnp.concatenate([decay_ref[...]] * (8 // heads), axis=0)
    lane = lax.broadcasted_iota(jnp.int32, running.shape, 1)
    shift = 1
    while shift < length:
        running += jnp.where(lane >= shift, pltpu.roll(running, shift, 1), 0.0)
        shift *= 2
    running_ref[...] = running
    column = running.T
    copies[1].wait()
    copies[2].wait()
    for h in range(heads):
        cols = slice(128 * h, 128 * h + 128)
        total = column[length - 1 : length, h : h + 1]
        weight = jnp.exp(total - column[:, h : h + 1])
        high, low = split(k_ref[:, cols].astype(F32) * weight)
        values = v_ref[:, cols]
        state = dot(high, values, TN) + dot(low, values, TN)
        chunks_ref[8 * h : 8 * h + 8, 0:16, 0, :] = state.reshape(8, 16, 128)
        chunks_ref[8 * h : 8 * h + 8, 16, 0, :] = jnp.broadcast_to(total, (8, 128))


def prefix_kernel(parent_ref, all_ref, out_ref):
    segments = all_ref.shape[0]
    for s in range(segments):
        first = parent_ref[s]
        p = jnp.clip(first, 0, segments - 1)
        second = parent_ref[p]
        g = jnp.clip(second, 0, segments - 1)
        own = all_ref[p, 0:16, 0, :]
        factor = jnp.exp(all_ref[p, 16:17, 0, :])
        older = jnp.where(second >= 0, factor * all_ref[g, 0:16, 0, :], 0.0)
        out_ref[s] = jnp.where(first >= 0, own + older, 0.0)


def within_kernel(first, q_hbm, k_hbm, v_hbm, running_ref, out_ref, q_ref, k_ref, v_ref, sems):
    copies = load(sems, (q_hbm, q_ref), (k_hbm, k_ref), (v_hbm, v_ref))
    length = q_ref.shape[0]
    size = 256
    scale = 128 ** (-0.5)
    causal = lax.broadcasted_iota(jnp.int32, (size, size), 0) >= lax.broadcasted_iota(jnp.int32, (size, size), 1)
    column = running_ref[...].T
    for copy in copies:
        copy.wait()
    for h in range(first, first + 2):
        cols = slice(128 * h, 128 * h + 128)
        for i in range(length // size):
            rows = slice(size * i, size * i + size)
            q = q_ref[rows, cols]
            total = None
            for j in range(i + 1):
                inner = slice(size * j, size * j + size)
                scores = dot(q, k_ref[inner, cols], NT)
                gap = column[rows, h : h + 1] - running_ref[h : h + 1, inner]
                factor = jnp.exp(jnp.minimum(gap, 0.0))
                if i == j:
                    factor = jnp.where(causal, factor, 0.0)
                weights = (scores * scale * factor).astype(BF16)
                term = dot(weights, v_ref[inner, cols])
                total = term if total is None else total + term
            out_ref[rows, cols.start - 128 * first : cols.stop - 128 * first] = total


def mix_kernel(
    place_ref, q_hbm, prefix_ref, early_ref, late_ref, running_ref, gain_ref, _,
    out_ref, squares_out_ref,
    q_ref, sems,
):
    heads = [slice(128 * h, 128 * h + 128) for h in range(4)]
    inputs = load(sems, *[(q_hbm.at[:, cols], q_ref.at[:, cols]) for cols in heads])
    parts, share, width = out_ref.shape
    growth = jnp.exp(running_ref[...].T)
    squares = None
    for h in range(4):
        cols = slice(128 * h, 128 * h + 128)
        high, low = split(prefix_ref[h])
        inputs[h].wait()
        q = q_ref[:, cols]
        inner = (early_ref if h < 2 else late_ref)[:, 128 * (h % 2) : 128 * (h % 2) + 128]
        both = dot(q, jnp.concatenate([high, low], axis=1))
        attention = (both[:, :128] + both[:, 128:]) * growth[:, h : h + 1] + inner
        term = jnp.sum(attention * attention, axis=1, keepdims=True)
        squares = term if squares is None else squares + term
        features = (attention * gain_ref[:, cols]).astype(BF16).reshape(parts, share, 128)
        for i in range(parts):
            out_ref[place_ref[i], :, cols] = features[i]
    squares = jnp.broadcast_to(squares, (parts * share, 128)).reshape(parts, share, 128)
    for i in range(parts):
        squares_out_ref[place_ref[i]] = squares[i]


def project_kernel(start, size, first, features_ref, squares_ref, w_ref, *refs):
    keep_ref, send_ref = refs[-2:]
    count, rows = keep_ref.shape[:2]
    sides = [slice(first, first + count), slice(4 + first, 4 + first + count)]
    left = jnp.concatenate([features_ref[side].reshape(count * rows, -1) for side in sides], axis=0)
    for n in range(0, size, 512):
        t = slice(n, n + 512)
        both = dot(left, w_ref[:, start + n : start + n + 512])
        keep_ref[:, :, t] = both[: count * rows].reshape(count, rows, 512)
        send_ref[:, :, t] = both[count * rows :].reshape(count, rows, 512)
    if keep_ref.shape[2] > size:
        keep_ref[:, :, size:] = squares_ref[sides[0]]
        send_ref[:, :, size:] = squares_ref[sides[1]]


def finish_kernel(start, extra, features, *refs):
    mine_ref, arrived_ref = refs[:2]
    if extra:
        out_hbm, inverse_ref, buffer, sems = refs[2:]
        width = mine_ref.shape[1] - extra
        inverse_ref[...] = 1.0 / jnp.sqrt((mine_ref[:, width:] + arrived_ref[:, width:]) / features + 1e-06)
    else:
        inverse_ref, _, out_hbm, buffer, sems = refs[2:]
        width = mine_ref.shape[1]
    inverse = inverse_ref[:, 0:1]
    tile = 512
    copies = []
    for i, n in enumerate(range(0, width, tile)):
        cols = slice(n, n + tile)
        buffer[:, cols] = ((mine_ref[:, cols] + arrived_ref[:, cols]) * inverse).astype(BF16)
        copy = pltpu.make_async_copy(buffer.at[:, cols], out_hbm.at[:, start + n : start + n + tile], sems.at[i])
        copy.start()
        copies.append(copy)
    for copy in copies:
        copy.wait()


VMEM = pl.BlockSpec(memory_space=pltpu.VMEM)
SMEM = pl.BlockSpec(memory_space=pltpu.SMEM)
ANY = pl.BlockSpec(memory_space=pl.ANY)
HBM = pl.BlockSpec(memory_space=pltpu.HBM)


def call(kernel, shapes, ins, outs=None, scratch=(), aliases=None, flops=2**28, moved=2**20, vmem=6 * 2**20):
    return pl.pallas_call(
        kernel,
        out_shape=[jax.ShapeDtypeStruct(s, d) for s, d in shapes],
        in_specs=ins,
        out_specs=outs or [VMEM] * len(shapes),
        scratch_shapes=list(scratch),
        input_output_aliases=aliases or {},
        compiler_params=pltpu.CompilerParams(vmem_limit_bytes=vmem),
        cost_estimate=pl.CostEstimate(flops=flops, bytes_accessed=moved, transcendentals=0),
    )


def head_pairs(target):
    pairs = []
    for y in range(4):
        for core in range(2):
            to, to_core = target(y, core)
            pairs.append((2 * y + core, 2 * (to % 4) + to_core))
    return pairs


SWAP = head_pairs(lambda y, core: (y, 1 - core))
RING = head_pairs(lambda y, core: (y + 1 - 2 * core, core))

def per_device(q, k, v, log_decay, parent, gain, w):
    length, width = q.shape
    dma = pltpu.SemaphoreType.DMA
    chunks, running = call(
        state_kernel,
        [((32, 17, 1, 128), F32), ((8, length), F32)],
        [HBM] * 3,
        scratch=[pltpu.VMEM(log_decay.shape, F32), pltpu.VMEM(k.shape, BF16), pltpu.VMEM(v.shape, BF16), dma((3,))],
        vmem=253 * 2**18,
    )(log_decay, k, v)
    everyone = lax.all_to_all(chunks, "seg", 0, 0, tiled=True)
    inputs = [pltpu.VMEM(q.shape, BF16)] * 3 + [dma((3,))]
    (early,) = call(
        functools.partial(within_kernel, 0), [((length, width // 2), F32)], [HBM] * 3 + [VMEM], scratch=inputs, flops=2**30
    )(q, k, v, running)
    everyone, early, running = lax.optimization_barrier((everyone, early, running))
    (mine,) = call(prefix_kernel, [((32, 16, 128), F32)], [SMEM, VMEM])(parent, everyone)
    prefix = lax.all_to_all(mine, "seg", 0, 0, tiled=True).reshape(4, 128, 128)
    (late,) = call(
        functools.partial(within_kernel, 2), [((length, width // 2), F32)], [HBM] * 3 + [VMEM], scratch=inputs, flops=2**30, vmem=62*2**20
    )(q, k, v, running)
    me = lax.axis_index("head")
    y, core = me >> 1, me & 1
    block = jnp.arange(8, dtype=jnp.int32)
    steps = (y - (block >> 1)) * (1 - 2 * core)
    places = jnp.where((block & 1) == core, (steps - 1) & 3, 4 + ((-steps - 1) & 3))
    share = length // 8
    starts = [0, 1536, 3584]
    widths = [1536, 2048, 2560]
    extras = [128, 0, 0]

    features, squares = call(
        mix_kernel,
        [((8, share, width), BF16), ((8, share, 128), F32)],
        [SMEM, HBM, VMEM, VMEM, VMEM, VMEM, VMEM, HBM],
        scratch=[pltpu.VMEM(q.shape, BF16), dma((4,))],
        flops=2**34,
        vmem=50 * 2**20,
    )(places, q, prefix, early, late, running, gain.reshape(1, width), w)

    def project(start, size, extra, first, after):
        return call(
            functools.partial(project_kernel, start, size, first),
            [((1, share, size + extra), F32)] * 2,
            [VMEM, VMEM, VMEM] + [ANY] * len(after),

        )(features, squares, w, *after)

    before, arrived = [], []
    for step in range(4):
        totals = []
        for i, (start, size, extra) in enumerate(zip(starts, widths, extras)):
            keep, send = project(start, size, extra, step, before if step == 1 else before[i : i + 1] if step > 1 else [])
            totals.append(keep[0] + lax.ppermute(send[0], "head", SWAP) + (arrived[i] if step in (1, 2) else 0.0))
        if step < 3:
            before = totals if step == 0 else arrived
            arrived = [lax.ppermute(total, "head", RING) for total in totals]
    total_features = width * lax.axis_size("head")
    out = ((share, w.shape[1]), BF16)
    for extra, start, size, i in sorted(zip(extras, starts, widths, range(len(starts))), key=lambda c: -c[0]):
        buffers = [pltpu.VMEM((share, size), BF16), dma((size // 512,))]
        kernel = functools.partial(finish_kernel, start, extra, total_features)
        terms = [totals[i], arrived[i]]
        if extra:
            mixed, inverse = call(kernel, [out, ((share, 128), F32)], [VMEM] * 2, outs=[ANY, VMEM], scratch=buffers)(*terms)
        else:
            (mixed,) = call(kernel, [out], [VMEM] * 3 + [ANY], outs=[ANY], scratch=buffers, aliases={3: 0})(
                *terms, inverse, mixed
            )
    return mixed


def solution(mesh):
    return jax.shard_map(
        per_device,
        mesh=mesh,
        in_specs=(P("seg", "head"), P("seg", "head"), P("seg", "head"), P("head", "seg"), P(), P("head"), P("head", None)),
        out_specs=P(("seg", "head"), None),
        check_vma=False,
    )
```

```python
import functools
import jax
import jax.numpy as jnp
from jax import lax
from jax.experimental import pallas as pl
from jax.experimental.pallas import tpu as pltpu
from jax.sharding import PartitionSpec as P

F32, BF16 = jnp.float32, jnp.bfloat16
NT = (((1,), (1,)), ((), ()))
TN = (((0,), (0,)), ((), ()))
NN = (((1,), (0,)), ((), ()))


def dot(a, b, dims=NN):
    return lax.dot_general(a, b, dims, preferred_element_type=F32)


def split(x):
    high = x.astype(BF16)
    return high, (x - high.astype(F32)).astype(BF16)


def load(sems, *pairs):
    copies = [pltpu.make_async_copy(source, target, sems.at[i]) for i, (source, target) in enumerate(pairs)]
    for copy in copies:
        copy.start()
    return copies


def state_kernel(decay_hbm, k_hbm, v_hbm, chunks_ref, running_ref, decay_ref, k_ref, v_ref, sems):
    copies = load(sems, (decay_hbm, decay_ref), (k_hbm, k_ref), (v_hbm, v_ref))
    copies[0].wait()
    heads, length = decay_ref.shape
    running = jnp.concatenate([decay_ref[...]] * (8 // heads), axis=0)
    lane = lax.broadcasted_iota(jnp.int32, running.shape, 1)
    shift = 1
    while shift < length:
        running += jnp.where(lane >= shift, pltpu.roll(running, shift, 1), 0.0)
        shift *= 2
    running_ref[...] = running
    column = running.T
    copies[1].wait()
    copies[2].wait()
    for h in range(heads):
        cols = slice(128 * h, 128 * h + 128)
        total = column[length - 1 : length, h : h + 1]
        weight = jnp.exp(total - column[:, h : h + 1])
        high, low = split(k_ref[:, cols].astype(F32) * weight)
        values = v_ref[:, cols]
        both = dot(values, jnp.concatenate([high, low], axis=1), TN)
        state = (both[:, :128] + both[:, 128:]).T
        chunks_ref[8 * h : 8 * h + 8, 0:16, 0, :] = state.reshape(8, 16, 128)
        chunks_ref[8 * h : 8 * h + 8, 16, 0, :] = jnp.broadcast_to(total, (8, 128))


def prefix_kernel(parent_ref, all_ref, out_ref):
    segments = all_ref.shape[0]
    for s in range(segments):
        first = parent_ref[s]
        p = jnp.clip(first, 0, segments - 1)
        second = parent_ref[p]
        g = jnp.clip(second, 0, segments - 1)
        own = all_ref[p, 0:16, 0, :]
        factor = jnp.exp(all_ref[p, 16:17, 0, :])
        older = jnp.where(second >= 0, factor * all_ref[g, 0:16, 0, :], 0.0)
        out_ref[s] = jnp.where(first >= 0, own + older, 0.0)


def within_kernel(first, q_hbm, k_hbm, v_hbm, running_ref, out_ref, q_ref, k_ref, v_ref, sems):
    copies = load(sems, (q_hbm, q_ref), (k_hbm, k_ref), (v_hbm, v_ref))
    length = q_ref.shape[0]
    size = 256
    scale = 128 ** (-0.5)
    causal = lax.broadcasted_iota(jnp.int32, (size, size), 0) >= lax.broadcasted_iota(jnp.int32, (size, size), 1)
    column = running_ref[...].T
    for copy in copies:
        copy.wait()
    for h in range(first, first + 2):
        cols = slice(128 * h, 128 * h + 128)
        for i in range(length // size):
            rows = slice(size * i, size * i + size)
            q = q_ref[rows, cols]
            total = None
            for j in range(i + 1):
                inner = slice(size * j, size * j + size)
                scores = dot(q, k_ref[inner, cols], NT)
                gap = column[rows, h : h + 1] - running_ref[h : h + 1, inner]
                factor = jnp.exp(jnp.minimum(gap, 0.0))
                if i == j:
                    factor = jnp.where(causal, factor, 0.0)
                weights = (scores * scale * factor).astype(BF16)
                term = dot(weights, v_ref[inner, cols])
                total = term if total is None else total + term
            out_ref[rows, cols.start - 128 * first : cols.stop - 128 * first] = total


def mix_kernel(
    place_ref, q_hbm, prefix_ref, early_ref, late_ref, running_ref, gain_ref, _,
    out_ref, squares_out_ref,
    q_ref, sems,
):
    heads = [slice(128 * h, 128 * h + 128) for h in range(4)]
    inputs = load(sems, *[(q_hbm.at[:, cols], q_ref.at[:, cols]) for cols in heads])
    parts, share, width = out_ref.shape
    growth = jnp.exp(running_ref[...].T)
    squares = None
    for h in range(4):
        cols = slice(128 * h, 128 * h + 128)
        high, low = split(prefix_ref[h])
        inputs[h].wait()
        q = q_ref[:, cols]
        inner = (early_ref if h < 2 else late_ref)[:, 128 * (h % 2) : 128 * (h % 2) + 128]
        both = dot(q, jnp.concatenate([high, low], axis=1))
        attention = (both[:, :128] + both[:, 128:]) * growth[:, h : h + 1] + inner
        term = jnp.sum(attention * attention, axis=1, keepdims=True)
        squares = term if squares is None else squares + term
        features = (attention * gain_ref[:, cols]).astype(BF16).reshape(parts, share, 128)
        for i in range(parts):
            out_ref[place_ref[i], :, cols] = features[i]
    squares = jnp.broadcast_to(squares, (parts * share, 128)).T[0:8, :]
    squares_out_ref[...] = jnp.zeros_like(squares_out_ref)
    for i in range(parts):
        squares_out_ref[place_ref[i], :, 0:share] = squares[:, share * i : share * i + share]


def project_kernel(start, size, step, features_ref, squares_ref, w_ref, *refs):
    keep_ref, send_ref = refs[-2:]
    rows = features_ref.shape[1]
    left = jnp.concatenate([features_ref[step], features_ref[4 + step]], axis=0)
    for n in range(0, size, 512):
        both = dot(left, w_ref[:, start + n : start + n + 512])
        for m in range(0, 512, 128):
            place = slice((n + m) // 128 * rows, (n + m) // 128 * rows + rows)
            keep_ref[place, :] = both[:rows, m : m + 128]
            send_ref[place, :] = both[rows:, m : m + 128]
    end = size // 128 * rows
    if keep_ref.shape[0] > end:
        keep_ref[end:, :] = squares_ref[step]
        send_ref[end:, :] = squares_ref[4 + step]


def finish_kernel(start, extra, features, *refs):
    mine_ref, arrived_ref = refs[:2]
    if extra:
        out_hbm, inverse_ref, buffer, sems = refs[2:]
        end = mine_ref.shape[0] - extra
        squares = mine_ref[end:, :] + arrived_ref[end:, :]
        column = jnp.broadcast_to(squares[0:1, :], (128, 128)).T[: inverse_ref.shape[0], :]
        inverse_ref[...] = 1.0 / jnp.sqrt(column / features + 1e-06)
    else:
        inverse_ref, _, out_hbm, buffer, sems = refs[2:]
    rows, width = buffer.shape
    inverse = inverse_ref[...]
    tile = 512
    copies = []
    for i, n in enumerate(range(0, width, tile)):
        for m in range(n, n + tile, 128):
            place = slice(m // 128 * rows, m // 128 * rows + rows)
            buffer[:, m : m + 128] = ((mine_ref[place, :] + arrived_ref[place, :]) * inverse).astype(BF16)
        copy = pltpu.make_async_copy(buffer.at[:, n : n + tile], out_hbm.at[:, start + n : start + n + tile], sems.at[i])
        copy.start()
        copies.append(copy)
    for copy in copies:
        copy.wait()


VMEM = pl.BlockSpec(memory_space=pltpu.VMEM)
SMEM = pl.BlockSpec(memory_space=pltpu.SMEM)
ANY = pl.BlockSpec(memory_space=pl.ANY)
HBM = pl.BlockSpec(memory_space=pltpu.HBM)


def call(kernel, shapes, ins, outs=None, scratch=(), aliases=None, flops=2**28, moved=2**20, vmem=6 * 2**20):
    return pl.pallas_call(
        kernel,
        out_shape=[jax.ShapeDtypeStruct(s, d) for s, d in shapes],
        in_specs=ins,
        out_specs=outs or [VMEM] * len(shapes),
        scratch_shapes=list(scratch),
        input_output_aliases=aliases or {},
        compiler_params=pltpu.CompilerParams(vmem_limit_bytes=vmem),
        cost_estimate=pl.CostEstimate(flops=flops, bytes_accessed=moved, transcendentals=0),
    )


def head_pairs(target):
    pairs = []
    for y in range(4):
        for core in range(2):
            to, to_core = target(y, core)
            pairs.append((2 * y + core, 2 * (to % 4) + to_core))
    return pairs


SWAP = head_pairs(lambda y, core: (y, 1 - core))
RING = head_pairs(lambda y, core: (y + 1 - 2 * core, core))

def per_device(q, k, v, log_decay, parent, gain, w):
    length, width = q.shape
    dma = pltpu.SemaphoreType.DMA
    chunks, running = call(
        state_kernel,
        [((32, 17, 1, 128), F32), ((8, length), F32)],
        [HBM] * 3,
        scratch=[pltpu.VMEM(log_decay.shape, F32), pltpu.VMEM(k.shape, BF16), pltpu.VMEM(v.shape, BF16), dma((3,))],
        vmem=253 * 2**18,
    )(log_decay, k, v)
    everyone = lax.all_to_all(chunks, "seg", 0, 0, tiled=True)
    inputs = [pltpu.VMEM(q.shape, BF16)] * 3 + [dma((3,))]
    (early,) = call(
        functools.partial(within_kernel, 0), [((length, width // 2), F32)], [HBM] * 3 + [VMEM], scratch=inputs, flops=2**30
    )(q, k, v, running)
    everyone, early, running = lax.optimization_barrier((everyone, early, running))
    (mine,) = call(prefix_kernel, [((32, 16, 128), F32)], [SMEM, VMEM])(parent, everyone)
    prefix = lax.all_to_all(mine, "seg", 0, 0, tiled=True).reshape(4, 128, 128)
    (late,) = call(
        functools.partial(within_kernel, 2), [((length, width // 2), F32)], [HBM] * 3 + [VMEM], scratch=inputs, flops=2**30, vmem=62*2**20
    )(q, k, v, running)
    me = lax.axis_index("head")
    y, core = me >> 1, me & 1
    block = jnp.arange(8, dtype=jnp.int32)
    steps = (y - (block >> 1)) * (1 - 2 * core)
    places = jnp.where((block & 1) == core, (steps - 1) & 3, 4 + ((-steps - 1) & 3))
    share = length // 8
    starts = [0, 1536, 3584]
    widths = [1536, 2048, 2560]
    extras = [8, 0, 0]

    features, squares = call(
        mix_kernel,
        [((8, share, width), BF16), ((8, 8, 128), F32)],
        [SMEM, HBM, VMEM, VMEM, VMEM, VMEM, VMEM, HBM],
        scratch=[pltpu.VMEM(q.shape, BF16), dma((4,))],
        flops=2**34,
        vmem=52 * 2**20,
    )(places, q, prefix, early, late, running, gain.reshape(1, width), w)

    def project(start, size, extra, first, after):
        return call(
            functools.partial(project_kernel, start, size, first),
            [((size // 128 * share + extra, 128), F32)] * 2,
            [VMEM, VMEM, VMEM] + [ANY] * len(after),

        )(features, squares, w, *after)

    before, arrived = [], []
    for step in range(4):
        totals = []
        for i, (start, size, extra) in enumerate(zip(starts, widths, extras)):
            keep, send = project(start, size, extra, step, before if step == 1 else before[i : i + 1] if step > 1 else [])
            totals.append(keep + lax.ppermute(send, "head", SWAP) + (arrived[i] if step in (1, 2) else 0.0))
        if step < 3:
            before = totals if step == 0 else arrived
            arrived = [lax.ppermute(total, "head", RING) for total in totals]
    total_features = width * lax.axis_size("head")
    out = ((share, w.shape[1]), BF16)
    for extra, start, size, i in sorted(zip(extras, starts, widths, range(len(starts))), key=lambda c: -c[0]):
        buffers = [pltpu.VMEM((share, size), BF16), dma((size // 512,))]
        kernel = functools.partial(finish_kernel, start, extra, total_features)
        terms = [totals[i], arrived[i]]
        if extra:
            mixed, inverse = call(kernel, [out, ((share, 128), F32)], [VMEM] * 2, outs=[ANY, VMEM], scratch=buffers)(*terms)
        else:
            (mixed,) = call(kernel, [out], [VMEM] * 3 + [ANY], outs=[ANY], scratch=buffers, aliases={3: 0})(
                *terms, inverse, mixed
            )
    return mixed


def solution(mesh):
    return jax.shard_map(
        per_device,
        mesh=mesh,
        in_specs=(P("seg", "head"), P("seg", "head"), P("seg", "head"), P("head", "seg"), P(), P("head"), P("head", None)),
        out_specs=P(("seg", "head"), None),
        check_vma=False,
    )
```

```python
import functools
import jax
import jax.numpy as jnp
from jax import lax
from jax.experimental import pallas as pl
from jax.experimental.pallas import tpu as pltpu
from jax.sharding import PartitionSpec as P

F32, BF16 = jnp.float32, jnp.bfloat16
NT = (((1,), (1,)), ((), ()))
TN = (((0,), (0,)), ((), ()))
NN = (((1,), (0,)), ((), ()))


def dot(a, b, dims=NN):
    return lax.dot_general(a, b, dims, preferred_element_type=F32)


def split(x):
    high = x.astype(BF16)
    return high, (x - high.astype(F32)).astype(BF16)


def load(sems, *pairs):
    copies = [pltpu.make_async_copy(source, target, sems.at[i]) for i, (source, target) in enumerate(pairs)]
    for copy in copies:
        copy.start()
    return copies


def state_kernel(decay_hbm, k_hbm, v_hbm, chunks_ref, running_ref, decay_ref, k_ref, v_ref, sems):
    copies = load(sems, (decay_hbm, decay_ref), (k_hbm, k_ref), (v_hbm, v_ref))
    copies[0].wait()
    heads, length = decay_ref.shape
    running = jnp.concatenate([decay_ref[...]] * (8 // heads), axis=0)
    lane = lax.broadcasted_iota(jnp.int32, running.shape, 1)
    shift = 1
    while shift < length:
        running += jnp.where(lane >= shift, pltpu.roll(running, shift, 1), 0.0)
        shift *= 2
    running_ref[...] = running
    column = running.T
    copies[1].wait()
    copies[2].wait()
    for h in range(heads):
        cols = slice(128 * h, 128 * h + 128)
        total = column[length - 1 : length, h : h + 1]
        weight = jnp.exp(total - column[:, h : h + 1])
        high, low = split(k_ref[:, cols].astype(F32) * weight)
        values = v_ref[:, cols]
        state = dot(high, values, TN) + dot(low, values, TN)
        chunks_ref[8 * h : 8 * h + 8, 0:16, 0, :] = state.reshape(8, 16, 128)
        chunks_ref[8 * h : 8 * h + 8, 16, 0, :] = jnp.broadcast_to(total, (8, 128))


def prefix_kernel(parent_ref, all_ref, out_ref):
    segments = all_ref.shape[0]
    for s in range(segments):
        first = parent_ref[s]
        p = jnp.clip(first, 0, segments - 1)
        second = parent_ref[p]
        g = jnp.clip(second, 0, segments - 1)
        own = all_ref[p, 0:16, 0, :]
        factor = jnp.exp(all_ref[p, 16:17, 0, :])
        older = jnp.where(second >= 0, factor * all_ref[g, 0:16, 0, :], 0.0)
        out_ref[s] = jnp.where(first >= 0, own + older, 0.0)


def within_kernel(first, q_hbm, k_hbm, v_hbm, running_ref, out_ref, q_ref, k_ref, v_ref, sems):
    copies = load(sems, (q_hbm, q_ref), (k_hbm, k_ref), (v_hbm, v_ref))
    length = q_ref.shape[0]
    size = 256
    scale = 128 ** (-0.5)
    causal = lax.broadcasted_iota(jnp.int32, (size, size), 0) >= lax.broadcasted_iota(jnp.int32, (size, size), 1)
    column = running_ref[...].T
    for copy in copies:
        copy.wait()
    for h in range(first, first + 2):
        cols = slice(128 * h, 128 * h + 128)
        for i in range(length // size):
            rows = slice(size * i, size * i + size)
            q = q_ref[rows, cols]
            total = None
            for j in range(i + 1):
                inner = slice(size * j, size * j + size)
                scores = dot(q, k_ref[inner, cols], NT)
                gap = column[rows, h : h + 1] - running_ref[h : h + 1, inner]
                factor = jnp.exp(jnp.minimum(gap, 0.0))
                if i == j:
                    factor = jnp.where(causal, factor, 0.0)
                weights = (scores * scale * factor).astype(BF16)
                term = dot(weights, v_ref[inner, cols])
                total = term if total is None else total + term
            out_ref[rows, cols.start - 128 * first : cols.stop - 128 * first] = total


def mix_kernel(
    place_ref, q_hbm, prefix_ref, early_ref, late_ref, running_ref, gain_ref, _,
    out_ref, squares_out_ref,
    q_ref, sems,
):
    heads = [slice(128 * h, 128 * h + 128) for h in range(4)]
    inputs = load(sems, *[(q_hbm.at[:, cols], q_ref.at[:, cols]) for cols in heads])
    parts, share, width = out_ref.shape
    growth = jnp.exp(running_ref[...].T)
    squares = None
    for h in range(4):
        cols = slice(128 * h, 128 * h + 128)
        high, low = split(prefix_ref[h])
        inputs[h].wait()
        q = q_ref[:, cols]
        inner = (early_ref if h < 2 else late_ref)[:, 128 * (h % 2) : 128 * (h % 2) + 128]
        both = dot(q, jnp.concatenate([high, low], axis=1))
        attention = (both[:, :128] + both[:, 128:]) * growth[:, h : h + 1] + inner
        term = jnp.sum(attention * attention, axis=1, keepdims=True)
        squares = term if squares is None else squares + term
        features = (attention * gain_ref[:, cols]).astype(BF16).reshape(parts, share, 128)
        for i in range(parts):
            out_ref[place_ref[i], :, cols] = features[i]
    squares = jnp.broadcast_to(squares, (parts * share, 128)).T[0:8, :]
    squares_out_ref[...] = jnp.zeros_like(squares_out_ref)
    for i in range(parts):
        squares_out_ref[place_ref[i], :, 0:share] = squares[:, share * i : share * i + share]


def project_kernel(start, size, step, features_ref, squares_ref, w_ref, *refs):
    keep_ref, send_ref = refs[-2:]
    rows = features_ref.shape[1]
    left = jnp.concatenate([features_ref[step], features_ref[4 + step]], axis=0)
    for n in range(0, size, 512):
        both = dot(left, w_ref[:, start + n : start + n + 512])
        for m in range(0, 512, 128):
            place = slice((n + m) // 128 * rows, (n + m) // 128 * rows + rows)
            keep_ref[0, place, :] = both[:rows, m : m + 128]
            send_ref[0, place, :] = both[rows:, m : m + 128]
    end = size // 128 * rows
    if keep_ref.shape[1] > end:
        keep_ref[0, end:, :] = squares_ref[step]
        send_ref[0, end:, :] = squares_ref[4 + step]


def finish_kernel(start, extra, features, *refs):
    mine_ref, arrived_ref = refs[:2]
    if extra:
        out_hbm, inverse_ref, buffer, sems = refs[2:]
        end = mine_ref.shape[0] - extra
        squares = mine_ref[end:, :] + arrived_ref[end:, :]
        column = jnp.broadcast_to(squares[0:1, :], (128, 128)).T[: inverse_ref.shape[0], :]
        inverse_ref[...] = 1.0 / jnp.sqrt(column / features + 1e-06)
    else:
        inverse_ref, _, out_hbm, buffer, sems = refs[2:]
    rows, width = buffer.shape
    inverse = inverse_ref[...]
    tile = 512
    copies = []
    for i, n in enumerate(range(0, width, tile)):
        for m in range(n, n + tile, 128):
            place = slice(m // 128 * rows, m // 128 * rows + rows)
            buffer[:, m : m + 128] = ((mine_ref[place, :] + arrived_ref[place, :]) * inverse).astype(BF16)
        copy = pltpu.make_async_copy(buffer.at[:, n : n + tile], out_hbm.at[:, start + n : start + n + tile], sems.at[i])
        copy.start()
        copies.append(copy)
    for copy in copies:
        copy.wait()


VMEM = pl.BlockSpec(memory_space=pltpu.VMEM)
SMEM = pl.BlockSpec(memory_space=pltpu.SMEM)
ANY = pl.BlockSpec(memory_space=pl.ANY)
HBM = pl.BlockSpec(memory_space=pltpu.HBM)


def call(kernel, shapes, ins, outs=None, scratch=(), aliases=None, flops=2**28, moved=2**20, vmem=6 * 2**20):
    return pl.pallas_call(
        kernel,
        out_shape=[jax.ShapeDtypeStruct(s, d) for s, d in shapes],
        in_specs=ins,
        out_specs=outs or [VMEM] * len(shapes),
        scratch_shapes=list(scratch),
        input_output_aliases=aliases or {},
        compiler_params=pltpu.CompilerParams(vmem_limit_bytes=vmem),
        cost_estimate=pl.CostEstimate(flops=flops, bytes_accessed=moved, transcendentals=0),
    )


def head_pairs(target):
    pairs = []
    for y in range(4):
        for core in range(2):
            to, to_core = target(y, core)
            pairs.append((2 * y + core, 2 * (to % 4) + to_core))
    return pairs


SWAP = head_pairs(lambda y, core: (y, 1 - core))
RING = head_pairs(lambda y, core: (y + 1 - 2 * core, core))

def per_device(q, k, v, log_decay, parent, gain, w):
    length, width = q.shape
    dma = pltpu.SemaphoreType.DMA
    chunks, running = call(
        state_kernel,
        [((32, 17, 1, 128), F32), ((8, length), F32)],
        [HBM] * 3,
        scratch=[pltpu.VMEM(log_decay.shape, F32), pltpu.VMEM(k.shape, BF16), pltpu.VMEM(v.shape, BF16), dma((3,))],
        vmem=253 * 2**18,
    )(log_decay, k, v)
    everyone = lax.all_to_all(chunks, "seg", 0, 0, tiled=True)
    inputs = [pltpu.VMEM(q.shape, BF16)] * 3 + [dma((3,))]
    (early,) = call(
        functools.partial(within_kernel, 0), [((length, width // 2), F32)], [HBM] * 3 + [VMEM], scratch=inputs, flops=2**30
    )(q, k, v, running)
    everyone, early, running = lax.optimization_barrier((everyone, early, running))
    (mine,) = call(prefix_kernel, [((32, 16, 128), F32)], [SMEM, VMEM])(parent, everyone)
    prefix = lax.all_to_all(mine, "seg", 0, 0, tiled=True).reshape(4, 128, 128)
    (late,) = call(
        functools.partial(within_kernel, 2), [((length, width // 2), F32)], [HBM] * 3 + [VMEM], scratch=inputs, flops=2**30, vmem=62*2**20
    )(q, k, v, running)
    me = lax.axis_index("head")
    y, core = me >> 1, me & 1
    block = jnp.arange(8, dtype=jnp.int32)
    steps = (y - (block >> 1)) * (1 - 2 * core)
    places = jnp.where((block & 1) == core, (steps - 1) & 3, 4 + ((-steps - 1) & 3))
    share = length // 8
    starts = [0, 1536, 3584]
    widths = [1536, 2048, 2560]
    extras = [8, 0, 0]

    features, squares = call(
        mix_kernel,
        [((8, share, width), BF16), ((8, 8, 128), F32)],
        [SMEM, HBM, VMEM, VMEM, VMEM, VMEM, VMEM, HBM],
        scratch=[pltpu.VMEM(q.shape, BF16), dma((4,))],
        flops=2**34,
        vmem=50 * 2**20,
    )(places, q, prefix, early, late, running, gain.reshape(1, width), w)

    def project(start, size, extra, first, after):
        return call(
            functools.partial(project_kernel, start, size, first),
            [((1, size // 128 * share + extra, 128), F32)] * 2,
            [VMEM, VMEM, VMEM] + [ANY] * len(after),

        )(features, squares, w, *after)

    before, arrived = [], []
    for step in range(4):
        totals = []
        for i, (start, size, extra) in enumerate(zip(starts, widths, extras)):
            keep, send = project(start, size, extra, step, before if step == 1 else before[i : i + 1] if step > 1 else [])
            totals.append(keep[0] + lax.ppermute(send[0], "head", SWAP) + (arrived[i] if step in (1, 2) else 0.0))
        if step < 3:
            before = totals if step == 0 else arrived
            arrived = [lax.ppermute(total, "head", RING) for total in totals]
    total_features = width * lax.axis_size("head")
    out = ((share, w.shape[1]), BF16)
    for extra, start, size, i in sorted(zip(extras, starts, widths, range(len(starts))), key=lambda c: -c[0]):
        buffers = [pltpu.VMEM((share, size), BF16), dma((size // 512,))]
        kernel = functools.partial(finish_kernel, start, extra, total_features)
        terms = [totals[i], arrived[i]]
        if extra:
            mixed, inverse = call(kernel, [out, ((share, 128), F32)], [VMEM] * 2, outs=[ANY, VMEM], scratch=buffers)(*terms)
        else:
            (mixed,) = call(kernel, [out], [VMEM] * 3 + [ANY], outs=[ANY], scratch=buffers, aliases={3: 0})(
                *terms, inverse, mixed
            )
    return mixed


def solution(mesh):
    return jax.shard_map(
        per_device,
        mesh=mesh,
        in_specs=(P("seg", "head"), P("seg", "head"), P("seg", "head"), P("head", "seg"), P(), P("head"), P("head", None)),
        out_specs=P(("seg", "head"), None),
        check_vma=False,
    )
```

```python
import functools
import jax
import jax.numpy as jnp
from jax import lax
from jax.experimental import pallas as pl
from jax.experimental.pallas import tpu as pltpu
from jax.sharding import PartitionSpec as P

F32, BF16 = jnp.float32, jnp.bfloat16
NT = (((1,), (1,)), ((), ()))
TN = (((0,), (0,)), ((), ()))
NN = (((1,), (0,)), ((), ()))


def dot(a, b, dims=NN):
    return lax.dot_general(a, b, dims, preferred_element_type=F32)


def split(x):
    high = x.astype(BF16)
    return high, (x - high.astype(F32)).astype(BF16)


def load(sems, *pairs):
    copies = [pltpu.make_async_copy(source, target, sems.at[i]) for i, (source, target) in enumerate(pairs)]
    for copy in copies:
        copy.start()
    return copies


def state_kernel(decay_hbm, k_hbm, v_hbm, chunks_ref, running_ref, decay_ref, k_ref, v_ref, sems):
    copies = load(sems, (decay_hbm, decay_ref), (k_hbm, k_ref), (v_hbm, v_ref))
    copies[0].wait()
    heads, length = decay_ref.shape
    running = jnp.concatenate([decay_ref[...]] * (8 // heads), axis=0)
    lane = lax.broadcasted_iota(jnp.int32, running.shape, 1)
    shift = 1
    while shift < length:
        running += jnp.where(lane >= shift, pltpu.roll(running, shift, 1), 0.0)
        shift *= 2
    running_ref[...] = running
    column = running.T
    copies[1].wait()
    copies[2].wait()
    for h in range(heads):
        cols = slice(128 * h, 128 * h + 128)
        total = column[length - 1 : length, h : h + 1]
        weight = jnp.exp(total - column[:, h : h + 1])
        high, low = split(k_ref[:, cols].astype(F32) * weight)
        values = v_ref[:, cols]
        state = dot(high, values, TN) + dot(low, values, TN)
        chunks_ref[8 * h : 8 * h + 8, 0:16, 0, :] = state.reshape(8, 16, 128)
        chunks_ref[8 * h : 8 * h + 8, 16, 0, :] = jnp.broadcast_to(total, (8, 128))


def prefix_kernel(parent_ref, all_ref, out_ref):
    segments = all_ref.shape[0]
    for s in range(segments):
        first = parent_ref[s]
        p = jnp.clip(first, 0, segments - 1)
        second = parent_ref[p]
        g = jnp.clip(second, 0, segments - 1)
        own = all_ref[p, 0:16, 0, :]
        factor = jnp.exp(all_ref[p, 16:17, 0, :])
        older = jnp.where(second >= 0, factor * all_ref[g, 0:16, 0, :], 0.0)
        out_ref[s] = jnp.where(first >= 0, own + older, 0.0)


def within_kernel(first, q_hbm, k_hbm, v_hbm, running_ref, out_ref, q_ref, k_ref, v_ref, sems):
    copies = load(sems, (q_hbm, q_ref), (k_hbm, k_ref), (v_hbm, v_ref))
    length = q_ref.shape[0]
    size = 256
    scale = 128 ** (-0.5)
    causal = lax.broadcasted_iota(jnp.int32, (size, size), 0) >= lax.broadcasted_iota(jnp.int32, (size, size), 1)
    column = running_ref[...].T
    for copy in copies:
        copy.wait()
    for h in range(first, first + 2):
        cols = slice(128 * h, 128 * h + 128)
        for i in range(length // size):
            rows = slice(size * i, size * i + size)
            q = q_ref[rows, cols]
            total = None
            for j in range(i + 1):
                inner = slice(size * j, size * j + size)
                scores = dot(q, k_ref[inner, cols], NT)
                gap = column[rows, h : h + 1] - running_ref[h : h + 1, inner]
                factor = jnp.exp(jnp.minimum(gap, 0.0))
                if i == j:
                    factor = jnp.where(causal, factor, 0.0)
                weights = (scores * scale * factor).astype(BF16)
                term = dot(weights, v_ref[inner, cols])
                total = term if total is None else total + term
            out_ref[rows, cols.start - 128 * first : cols.stop - 128 * first] = total


def mix_kernel(
    place_ref, q_hbm, prefix_ref, early_hbm, late_ref, running_ref, gain_ref, _,
    out_ref, squares_out_ref,
    q_ref, early_ref, sems,
):
    heads = [slice(128 * h, 128 * h + 128) for h in range(4)]
    inputs = load(sems, *[(q_hbm.at[:, cols], q_ref.at[:, cols]) for cols in heads[2:] + heads[:2]], (early_hbm, early_ref))
    parts, share, width = out_ref.shape
    growth = jnp.exp(running_ref[...].T)
    squares = None
    for h in (2, 3, 0, 1):
        cols = heads[h]
        high, low = split(prefix_ref[h])
        inputs[(h + 2) % 4].wait()
        if h == 0:
            inputs[4].wait()
        q = q_ref[:, cols]
        inner = (early_ref if h < 2 else late_ref)[:, 128 * (h % 2) : 128 * (h % 2) + 128]
        both = dot(q, jnp.concatenate([high, low], axis=1))
        attention = (both[:, :128] + both[:, 128:]) * growth[:, h : h + 1] + inner
        term = jnp.sum(attention * attention, axis=1, keepdims=True)
        squares = term if squares is None else squares + term
        features = (attention * gain_ref[:, cols]).astype(BF16).reshape(parts, share, 128)
        for i in range(parts):
            out_ref[place_ref[i], :, cols] = features[i]
    squares = jnp.broadcast_to(squares, (parts * share, 128)).T[0:8, :]
    squares_out_ref[...] = jnp.zeros_like(squares_out_ref)
    for i in range(parts):
        squares_out_ref[place_ref[i], :, 0:share] = squares[:, share * i : share * i + share]


def project_kernel(start, size, step, features_ref, squares_ref, w_ref, *refs):
    keep_ref, send_ref = refs[-2:]
    rows = features_ref.shape[1]
    left = jnp.concatenate([features_ref[step], features_ref[4 + step]], axis=0)
    for n in range(0, size, 512):
        both = dot(left, w_ref[:, start + n : start + n + 512])
        for m in range(0, 512, 128):
            place = slice((n + m) // 128 * rows, (n + m) // 128 * rows + rows)
            keep_ref[0, place, :] = both[:rows, m : m + 128]
            send_ref[0, place, :] = both[rows:, m : m + 128]
    end = size // 128 * rows
    if keep_ref.shape[1] > end:
        keep_ref[0, end:, :] = squares_ref[step]
        send_ref[0, end:, :] = squares_ref[4 + step]


def finish_kernel(start, extra, features, *refs):
    mine_ref, arrived_ref = refs[:2]
    if extra:
        out_hbm, inverse_ref, buffer, sems = refs[2:]
        end = mine_ref.shape[0] - extra
        squares = mine_ref[end:, :] + arrived_ref[end:, :]
        column = jnp.broadcast_to(squares[0:1, :], (128, 128)).T[: inverse_ref.shape[0], :]
        inverse_ref[...] = 1.0 / jnp.sqrt(column / features + 1e-06)
    else:
        inverse_ref, _, out_hbm, buffer, sems = refs[2:]
    rows, width = buffer.shape
    inverse = inverse_ref[...]
    tile = 512
    copies = []
    for i, n in enumerate(range(0, width, tile)):
        for m in range(n, n + tile, 128):
            place = slice(m // 128 * rows, m // 128 * rows + rows)
            buffer[:, m : m + 128] = ((mine_ref[place, :] + arrived_ref[place, :]) * inverse).astype(BF16)
        copy = pltpu.make_async_copy(buffer.at[:, n : n + tile], out_hbm.at[:, start + n : start + n + tile], sems.at[i])
        copy.start()
        copies.append(copy)
    for copy in copies:
        copy.wait()


VMEM = pl.BlockSpec(memory_space=pltpu.VMEM)
SMEM = pl.BlockSpec(memory_space=pltpu.SMEM)
ANY = pl.BlockSpec(memory_space=pl.ANY)
HBM = pl.BlockSpec(memory_space=pltpu.HBM)


def call(kernel, shapes, ins, outs=None, scratch=(), aliases=None, flops=2**28, moved=2**20, vmem=6 * 2**20):
    return pl.pallas_call(
        kernel,
        out_shape=[jax.ShapeDtypeStruct(s, d) for s, d in shapes],
        in_specs=ins,
        out_specs=outs or [VMEM] * len(shapes),
        scratch_shapes=list(scratch),
        input_output_aliases=aliases or {},
        compiler_params=pltpu.CompilerParams(vmem_limit_bytes=vmem),
        cost_estimate=pl.CostEstimate(flops=flops, bytes_accessed=moved, transcendentals=0),
    )


def head_pairs(target):
    pairs = []
    for y in range(4):
        for core in range(2):
            to, to_core = target(y, core)
            pairs.append((2 * y + core, 2 * (to % 4) + to_core))
    return pairs


SWAP = head_pairs(lambda y, core: (y, 1 - core))
RING = head_pairs(lambda y, core: (y + 1 - 2 * core, core))

def per_device(q, k, v, log_decay, parent, gain, w):
    length, width = q.shape
    dma = pltpu.SemaphoreType.DMA
    chunks, running = call(
        state_kernel,
        [((32, 17, 1, 128), F32), ((8, length), F32)],
        [HBM] * 3,
        scratch=[pltpu.VMEM(log_decay.shape, F32), pltpu.VMEM(k.shape, BF16), pltpu.VMEM(v.shape, BF16), dma((3,))],
        vmem=253 * 2**18,
    )(log_decay, k, v)
    everyone = lax.all_to_all(chunks, "seg", 0, 0, tiled=True)
    inputs = [pltpu.VMEM(q.shape, BF16)] * 3 + [dma((3,))]
    (early,) = call(
        functools.partial(within_kernel, 0), [((length, width // 2), F32)], [HBM] * 3 + [VMEM], scratch=inputs, flops=2**30
    )(q, k, v, running)
    everyone, early, running = lax.optimization_barrier((everyone, early, running))
    (mine,) = call(prefix_kernel, [((32, 16, 128), F32)], [SMEM, VMEM])(parent, everyone)
    prefix = lax.all_to_all(mine, "seg", 0, 0, tiled=True).reshape(4, 128, 128)
    (late,) = call(
        functools.partial(within_kernel, 2), [((length, width // 2), F32)], [HBM] * 3 + [VMEM], scratch=inputs, flops=2**30, vmem=62*2**20
    )(q, k, v, running)
    me = lax.axis_index("head")
    y, core = me >> 1, me & 1
    block = jnp.arange(8, dtype=jnp.int32)
    steps = (y - (block >> 1)) * (1 - 2 * core)
    places = jnp.where((block & 1) == core, (steps - 1) & 3, 4 + ((-steps - 1) & 3))
    share = length // 8
    starts = [0, 1536, 3584]
    widths = [1536, 2048, 2560]
    extras = [8, 0, 0]

    features, squares = call(
        mix_kernel,
        [((8, share, width), BF16), ((8, 8, 128), F32)],
        [SMEM, HBM, VMEM, HBM, VMEM, VMEM, VMEM, HBM],
        scratch=[pltpu.VMEM(q.shape, BF16), pltpu.VMEM(early.shape, F32), dma((5,))],
        flops=2**34,
        vmem=51 * 2**20,
    )(places, q, prefix, early, late, running, gain.reshape(1, width), w)

    def project(start, size, extra, first, after):
        return call(
            functools.partial(project_kernel, start, size, first),
            [((1, size // 128 * share + extra, 128), F32)] * 2,
            [VMEM, VMEM, VMEM] + [ANY] * len(after),

        )(features, squares, w, *after)

    before, arrived = [], []
    for step in range(4):
        totals = []
        for i, (start, size, extra) in enumerate(zip(starts, widths, extras)):
            keep, send = project(start, size, extra, step, before if step == 1 else before[i : i + 1] if step > 1 else [])
            totals.append(keep[0] + lax.ppermute(send[0], "head", SWAP) + (arrived[i] if step in (1, 2) else 0.0))
        if step < 3:
            before = totals if step == 0 else arrived
            arrived = [lax.ppermute(total, "head", RING) for total in totals]
    total_features = width * lax.axis_size("head")
    out = ((share, w.shape[1]), BF16)
    for extra, start, size, i in sorted(zip(extras, starts, widths, range(len(starts))), key=lambda c: -c[0]):
        buffers = [pltpu.VMEM((share, size), BF16), dma((size // 512,))]
        kernel = functools.partial(finish_kernel, start, extra, total_features)
        terms = [totals[i], arrived[i]]
        if extra:
            mixed, inverse = call(kernel, [out, ((share, 128), F32)], [VMEM] * 2, outs=[ANY, VMEM], scratch=buffers)(*terms)
        else:
            (mixed,) = call(kernel, [out], [VMEM] * 3 + [ANY], outs=[ANY], scratch=buffers, aliases={3: 0})(
                *terms, inverse, mixed
            )
    return mixed


def solution(mesh):
    return jax.shard_map(
        per_device,
        mesh=mesh,
        in_specs=(P("seg", "head"), P("seg", "head"), P("seg", "head"), P("head", "seg"), P(), P("head"), P("head", None)),
        out_specs=P(("seg", "head"), None),
        check_vma=False,
    )
```

```python
import functools
import jax
import jax.numpy as jnp
from jax import lax
from jax.experimental import pallas as pl
from jax.experimental.pallas import tpu as pltpu
from jax.sharding import PartitionSpec as P

F32, BF16 = jnp.float32, jnp.bfloat16
NT = (((1,), (1,)), ((), ()))
TN = (((0,), (0,)), ((), ()))
NN = (((1,), (0,)), ((), ()))


def dot(a, b, dims=NN):
    return lax.dot_general(a, b, dims, preferred_element_type=F32)


def split(x):
    high = x.astype(BF16)
    return high, (x - high.astype(F32)).astype(BF16)


def load(sems, *pairs):
    copies = [pltpu.make_async_copy(source, target, sems.at[i]) for i, (source, target) in enumerate(pairs)]
    for copy in copies:
        copy.start()
    return copies


def state_kernel(decay_hbm, k_hbm, v_hbm, chunks_ref, running_ref, decay_ref, k_ref, v_ref, sems):
    copies = load(sems, (decay_hbm, decay_ref), (k_hbm, k_ref), (v_hbm, v_ref))
    copies[0].wait()
    heads, length = decay_ref.shape
    running = jnp.concatenate([decay_ref[...]] * (8 // heads), axis=0)
    lane = lax.broadcasted_iota(jnp.int32, running.shape, 1)
    shift = 1
    while shift < length:
        running += jnp.where(lane >= shift, pltpu.roll(running, shift, 1), 0.0)
        shift *= 2
    running_ref[...] = running
    column = running.T
    copies[1].wait()
    copies[2].wait()
    for h in range(heads):
        cols = slice(128 * h, 128 * h + 128)
        total = column[length - 1 : length, h : h + 1]
        weight = jnp.exp(total - column[:, h : h + 1])
        high, low = split(k_ref[:, cols].astype(F32) * weight)
        values = v_ref[:, cols]
        state = dot(high, values, TN) + dot(low, values, TN)
        chunks_ref[8 * h : 8 * h + 8, 0:16, 0, :] = state.reshape(8, 16, 128)
        chunks_ref[8 * h : 8 * h + 8, 16, 0, :] = jnp.broadcast_to(total, (8, 128))


def prefix_kernel(parent_ref, all_ref, out_ref):
    segments = all_ref.shape[0]
    for s in range(segments):
        first = parent_ref[s]
        p = jnp.clip(first, 0, segments - 1)
        second = parent_ref[p]
        g = jnp.clip(second, 0, segments - 1)
        own = all_ref[p, 0:16, 0, :]
        factor = jnp.exp(all_ref[p, 16:17, 0, :])
        older = jnp.where(second >= 0, factor * all_ref[g, 0:16, 0, :], 0.0)
        out_ref[s] = jnp.where(first >= 0, own + older, 0.0)


def within_kernel(first, q_hbm, k_hbm, v_hbm, running_ref, out_ref, q_ref, k_ref, v_ref, sems):
    copies = load(sems, (q_hbm, q_ref), (k_hbm, k_ref), (v_hbm, v_ref))
    length = q_ref.shape[0]
    size = 256
    scale = 128 ** (-0.5)
    causal = lax.broadcasted_iota(jnp.int32, (size, size), 0) >= lax.broadcasted_iota(jnp.int32, (size, size), 1)
    column = running_ref[...].T
    for copy in copies:
        copy.wait()
    for h in range(first, first + 2):
        cols = slice(128 * h, 128 * h + 128)
        for i in range(length // size):
            rows = slice(size * i, size * i + size)
            q = q_ref[rows, cols]
            total = None
            for j in range(i + 1):
                inner = slice(size * j, size * j + size)
                scores = dot(q, k_ref[inner, cols], NT)
                gap = column[rows, h : h + 1] - running_ref[h : h + 1, inner]
                factor = jnp.exp(jnp.minimum(gap, 0.0))
                if i == j:
                    factor = jnp.where(causal, factor, 0.0)
                weights = (scores * scale * factor).astype(BF16)
                term = dot(weights, v_ref[inner, cols])
                total = term if total is None else total + term
            out_ref[rows, cols.start - 128 * first : cols.stop - 128 * first] = total


def mix_kernel(
    place_ref, q_hbm, prefix_ref, early_ref, late_ref, running_ref, gain_ref, _,
    out_ref, squares_out_ref,
    q_ref, sems,
):
    heads = [slice(128 * h, 128 * h + 128) for h in range(4)]
    inputs = load(sems, *[(q_hbm.at[:, cols], q_ref.at[:, cols]) for cols in heads])
    parts, share, width = out_ref.shape
    growth = jnp.exp(running_ref[...].T)
    squares = None
    for h in range(4):
        cols = slice(128 * h, 128 * h + 128)
        high, low = split(prefix_ref[h])
        inputs[h].wait()
        q = q_ref[:, cols]
        inner = (early_ref if h < 2 else late_ref)[:, 128 * (h % 2) : 128 * (h % 2) + 128]
        both = dot(q, jnp.concatenate([high, low], axis=1))
        attention = (both[:, :128] + both[:, 128:]) * growth[:, h : h + 1] + inner
        term = jnp.sum(attention * attention, axis=1, keepdims=True)
        squares = term if squares is None else squares + term
        features = (attention * gain_ref[:, cols]).astype(BF16).reshape(parts, share, 128)
        for i in range(parts):
            out_ref[place_ref[i], :, cols] = features[i]
    squares = jnp.broadcast_to(squares, (parts * share, 128)).T[0:8, :]
    squares_out_ref[...] = jnp.zeros_like(squares_out_ref)
    for i in range(parts):
        squares_out_ref[place_ref[i], :, 0:share] = squares[:, share * i : share * i + share]


def project_kernel(start, size, step, features_ref, squares_ref, w_ref, *refs):
    keep_ref, send_ref = refs[-2:]
    rows = features_ref.shape[1]
    left = jnp.concatenate([features_ref[step], features_ref[4 + step]], axis=0)
    for n in range(0, size, 512):
        both = dot(left, w_ref[:, start + n : start + n + 512])
        for m in range(0, 512, 128):
            place = slice((n + m) // 128 * rows, (n + m) // 128 * rows + rows)
            keep_ref[0, place, :] = both[:rows, m : m + 128]
            send_ref[0, place, :] = both[rows:, m : m + 128]
    end = size // 128 * rows
    if keep_ref.shape[1] > end:
        keep_ref[0, end:, :] = squares_ref[step]
        send_ref[0, end:, :] = squares_ref[4 + step]


def finish_kernel(start, extra, features, *refs):
    mine_ref, arrived_ref = refs[:2]
    if extra:
        out_hbm, inverse_ref, buffer, sems = refs[2:]
        end = mine_ref.shape[0] - extra
        squares = mine_ref[end:, :] + arrived_ref[end:, :]
        column = jnp.broadcast_to(squares[0:1, :], (128, 128)).T[: inverse_ref.shape[0], :]
        inverse_ref[...] = 1.0 / jnp.sqrt(column / features + 1e-06)
    else:
        inverse_ref, _, out_hbm, buffer, sems = refs[2:]
    rows, width = buffer.shape
    inverse = inverse_ref[...]
    tile = 512
    copies = []
    for i, n in enumerate(range(0, width, tile)):
        for m in range(n, n + tile, 128):
            place = slice(m // 128 * rows, m // 128 * rows + rows)
            buffer[:, m : m + 128] = ((mine_ref[place, :] + arrived_ref[place, :]) * inverse).astype(BF16)
        copy = pltpu.make_async_copy(buffer.at[:, n : n + tile], out_hbm.at[:, start + n : start + n + tile], sems.at[i])
        copy.start()
        copies.append(copy)
    for copy in copies:
        copy.wait()


VMEM = pl.BlockSpec(memory_space=pltpu.VMEM)
SMEM = pl.BlockSpec(memory_space=pltpu.SMEM)
ANY = pl.BlockSpec(memory_space=pl.ANY)
HBM = pl.BlockSpec(memory_space=pltpu.HBM)


def call(kernel, shapes, ins, outs=None, scratch=(), aliases=None, flops=2**28, moved=2**20, vmem=6 * 2**20):
    return pl.pallas_call(
        kernel,
        out_shape=[jax.ShapeDtypeStruct(s, d) for s, d in shapes],
        in_specs=ins,
        out_specs=outs or [VMEM] * len(shapes),
        scratch_shapes=list(scratch),
        input_output_aliases=aliases or {},
        compiler_params=pltpu.CompilerParams(vmem_limit_bytes=vmem),
        cost_estimate=pl.CostEstimate(flops=flops, bytes_accessed=moved, transcendentals=0),
    )


def head_pairs(target):
    pairs = []
    for y in range(4):
        for core in range(2):
            to, to_core = target(y, core)
            pairs.append((2 * y + core, 2 * (to % 4) + to_core))
    return pairs


SWAP = head_pairs(lambda y, core: (y, 1 - core))
RING = head_pairs(lambda y, core: (y + 1 - 2 * core, core))

def per_device(q, k, v, log_decay, parent, gain, w):
    length, width = q.shape
    dma = pltpu.SemaphoreType.DMA
    chunks, running = call(
        state_kernel,
        [((32, 17, 1, 128), F32), ((8, length), F32)],
        [HBM] * 3,
        scratch=[pltpu.VMEM(log_decay.shape, F32), pltpu.VMEM(k.shape, BF16), pltpu.VMEM(v.shape, BF16), dma((3,))],
        vmem=253 * 2**18,
    )(log_decay, k, v)
    everyone = lax.all_to_all(chunks, "seg", 0, 0, tiled=True)
    inputs = [pltpu.VMEM(q.shape, BF16)] * 3 + [dma((3,))]
    (early,) = call(
        functools.partial(within_kernel, 0), [((length, width // 2), F32)], [HBM] * 3 + [VMEM], scratch=inputs, flops=2**30
    )(q, k, v, running)
    everyone, early, running = lax.optimization_barrier((everyone, early, running))
    (mine,) = call(prefix_kernel, [((32, 16, 128), F32)], [SMEM, VMEM])(parent, everyone)
    prefix = lax.all_to_all(mine, "seg", 0, 0, tiled=True).reshape(4, 128, 128)
    (late,) = call(
        functools.partial(within_kernel, 2), [((length, width // 2), F32)], [HBM] * 3 + [VMEM], scratch=inputs, flops=2**30, vmem=62*2**20
    )(q, k, v, running)
    me = lax.axis_index("head")
    y, core = me >> 1, me & 1
    block = jnp.arange(8, dtype=jnp.int32)
    steps = (y - (block >> 1)) * (1 - 2 * core)
    places = jnp.where((block & 1) == core, (steps - 1) & 3, 4 + ((-steps - 1) & 3))
    share = length // 8
    starts = [0, 1536, 3584]
    widths = [1536, 2048, 2560]
    extras = [8, 0, 0]

    features, squares = call(
        mix_kernel,
        [((8, share, width), BF16), ((8, 8, 128), F32)],
        [SMEM, HBM, VMEM, VMEM, VMEM, VMEM, VMEM, HBM],
        scratch=[pltpu.VMEM(q.shape, BF16), dma((4,))],
        flops=2**34,
        vmem=51 * 2**20,
    )(places, q, prefix, early, late, running, gain.reshape(1, width), w)

    def project(start, size, extra, first, after):
        return call(
            functools.partial(project_kernel, start, size, first),
            [((1, size // 128 * share + extra, 128), F32)] * 2,
            [VMEM, VMEM, VMEM] + [ANY] * len(after),

        )(features, squares, w, *after)

    before, arrived = [], []
    for step in range(4):
        totals = []
        for i, (start, size, extra) in enumerate(zip(starts, widths, extras)):
            keep, send = project(start, size, extra, step, before if step == 1 else before[i : i + 1] if step > 1 else [])
            totals.append(keep[0] + lax.ppermute(send[0], "head", SWAP) + (arrived[i] if step in (1, 2) else 0.0))
        if step < 3:
            before = totals if step == 0 else arrived
            arrived = [lax.ppermute(total, "head", RING) for total in totals]
    total_features = width * lax.axis_size("head")
    out = ((share, w.shape[1]), BF16)
    for extra, start, size, i in sorted(zip(extras, starts, widths, range(len(starts))), key=lambda c: -c[0]):
        buffers = [pltpu.VMEM((share, size), BF16), dma((size // 512,))]
        kernel = functools.partial(finish_kernel, start, extra, total_features)
        terms = [totals[i], arrived[i]]
        if extra:
            mixed, inverse = call(kernel, [out, ((share, 128), F32)], [VMEM] * 2, outs=[ANY, VMEM], scratch=buffers)(*terms)
        else:
            (mixed,) = call(kernel, [out], [VMEM] * 3 + [ANY], outs=[ANY], scratch=buffers, aliases={3: 0})(
                *terms, inverse, mixed
            )
    return mixed


def solution(mesh):
    return jax.shard_map(
        per_device,
        mesh=mesh,
        in_specs=(P("seg", "head"), P("seg", "head"), P("seg", "head"), P("head", "seg"), P(), P("head"), P("head", None)),
        out_specs=P(("seg", "head"), None),
        check_vma=False,
    )
```
